128 devices in a mesh: ctx: 16 (over x_lo, z, core), tp: 8 (over x_hi, y).
Axes of the slice: x: 4 (x_hi: 2, x_lo: 2; x = x_hi * 2 + x_lo), y: 4, z: 4, core: 2. Of those that a mesh axis runs over, the one named last changes fastest.
Arguments:
- fine_x: bfloat16 [16384, 8192], P(('ctx', 'tp')), may hold values from -6 to 6
- fine_q: bfloat16 [16384, 8192], P(('ctx', 'tp'))
- fine_k: bfloat16 [16384, 1024], P(('ctx', 'tp'))
- fine_v: bfloat16 [16384, 1024], P(('ctx', 'tp')), may hold values from -6 to 6
- windows: int32 [64], replicated, may hold values from 128 to 512, as said below
- pool_w: float32 [4, 8192], replicated, may hold values from -3 to 3
- norm_gain: float32 [8192], replicated, may hold values from 0.5 to 2
- w_query: bfloat16 [8192, 4096], P('ctx', 'tp')
- w_key: bfloat16 [8192, 1024], P('ctx', 'tp')
- w_value: bfloat16 [8192, 1024], P('ctx', 'tp'), may hold values from -0.0625 to 0.0625
- w_out: bfloat16 [4096, 8192], P('tp', 'ctx'), may hold values from -0.09375 to 0.09375
- up_w: float32 [4, 8192], replicated, may hold values from -3 to 3
Outputs:
- fine_out: float32 [16384, 8192], P(('ctx', 'tp'))
The draws below stay inside these ranges and needn't reach their ends.
Inputs may be any that keep to these rules, and one draw needn't show every extreme that they name: `windows`: one head's window is exactly 512.
All inputs are finite; a program needn't handle non-finite values.
Results may differ from the reference program's by a relative error of at most 0.011.
Values may be sent and summed in bfloat16 or wider, within the bound.
A program may use at most 128 MiB of HBM per device.

```python
import math
import jax
import jax.numpy as jnp
from jax import lax

D = 8192
HEAD = 128
HEADS_F = 64
KV = 8
HEADS_C = 32
WIN = 512
POOL = 4
TOKENS = 16384
COARSE = 4096


def base_keys(key):
    drawn = jax.random.normal(jax.random.fold_in(key, 102), (TOKENS, KV * HEAD), jnp.float32)
    return jnp.clip(drawn, -6.0, 6.0)


def base_query(key):
    drawn = jax.random.normal(jax.random.fold_in(key, 201), (D, HEADS_C * HEAD), jnp.float32)
    return jnp.clip(drawn, -6.0, 6.0) * D ** (-0.5)


def draw_fine_k(key, part):
    keys_drawn = base_keys(key)
    return keys_drawn.astype(jnp.bfloat16)


def draw_fine_q(key, part):
    key = jax.random.fold_in(key, 2)
    queries = jnp.clip(jax.random.normal(key, (TOKENS, HEADS_F * HEAD), jnp.float32), -6.0, 6.0)
    return queries.astype(jnp.bfloat16)


def draw_windows(key, part):
    key = jax.random.fold_in(key, 4)
    spans = jax.random.randint(key, (HEADS_F,), WIN // 4, WIN + 1)
    chosen = jax.random.randint(jax.random.fold_in(key, 5), (), 0, HEADS_F)
    return jnp.where(jnp.arange(HEADS_F) == chosen, WIN, spans).astype(jnp.int32)


def draw_w_query(key, part):
    weights = base_query(key)
    return (weights * 2.0).astype(jnp.bfloat16)


def draw_w_key(key, part):
    key = jax.random.fold_in(key, 7)
    drawn = jnp.clip(jax.random.normal(key, (D, KV * HEAD), jnp.float32), -6.0, 6.0) * D ** (-0.5)
    return (drawn * 2.0).astype(jnp.bfloat16)


def levels(key, extent, cuts, smallest, top_value):
    def one(dim, blocks):
        draws = jax.random.uniform(jax.random.fold_in(jax.random.fold_in(key, 6), dim), (blocks,), jnp.float32, smallest / len(cuts), top_value / len(cuts))
        return jnp.repeat(jnp.exp(draws), extent[dim] // blocks).reshape((-1,) + (1,) * (len(extent) - dim - 1))

    gain = one(*cuts[0])
    for cut in cuts[1:]:
        gain = gain * one(*cut)
    return gain


def scatter_about(stream_key, shape, deviation, reach, cuts=(), held_as=jnp.bfloat16):
    array = jax.random.normal(stream_key, shape, jnp.float32) * deviation
    if len(cuts) > 0:
        array = levels(stream_key, shape, cuts, -0.22, 0.18) * array
    return jnp.clip(array, min=-reach, max=reach).astype(held_as)


def setup_inputs(seed: int = 0) -> dict:
    key_list = jax.random.split(jax.random.key(seed), 13)
    return {
        "fine_x": scatter_about(key_list[0], (TOKENS, D), 1.0, 6.0, ((0, 128),)),
        "fine_q": draw_fine_q(jax.random.fold_in(key_list[12], 71), 0),
        "fine_k": draw_fine_k(jax.random.fold_in(key_list[12], 71), 0),
        "fine_v": scatter_about(key_list[3], (TOKENS, KV * HEAD), 1.0, 6.0, ((0, 128),)),
        "windows": draw_windows(jax.random.fold_in(key_list[12], 71), 0),
        "pool_w": scatter_about(key_list[5], (POOL, D), 0.5, 3.0, (), jnp.float32),
        "norm_gain": jnp.clip(jnp.exp(jax.random.uniform(key_list[6], (D,), jnp.float32, math.log(0.5), math.log(2.0))), 0.5, 2.0),
        "w_query": draw_w_query(jax.random.fold_in(key_list[12], 71), 0),
        "w_key": draw_w_key(jax.random.fold_in(key_list[12], 71), 0),
        "w_value": scatter_about(key_list[9], (D, KV * HEAD), D ** -0.5, 0.0625, ((0, 16), (1, 8))),
        "w_out": scatter_about(key_list[10], (HEADS_C * HEAD, D), (HEADS_C * HEAD) ** -0.5, 0.09375, ((0, 8), (1, 16))),
        "up_w": scatter_about(key_list[11], (POOL, D), 0.5, 3.0, (), jnp.float32),
    }


def attend_window(queries, key_rows, value_rows, query_pos, key_pos, windows):
    group_size = queries.shape[2]
    scores = jnp.einsum('qkgd,lkd->kgql', queries.astype(jnp.float32), key_rows.astype(jnp.float32)) * HEAD ** (-0.5)
    distance = query_pos[:, None] - key_pos[None, :]
    spans = windows.reshape(KV, group_size, 1, 1)
    allowed = (distance[None, None] >= 0) & (distance[None, None] < spans) & (key_pos[None, None, None, :] >= 0)
    scores = jnp.where(allowed, scores, -1e+30)
    row_top = scores.max(-1, keepdims=True)
    weights = jnp.where(allowed, jnp.exp(scores - row_top), 0.0)
    row_total = weights.sum(-1)
    mixed_heads = jnp.einsum('kgql,lkd->qkgd', weights.astype(jnp.bfloat16).astype(jnp.float32), value_rows.astype(jnp.float32))
    return mixed_heads / jnp.transpose(row_total, (2, 0, 1))[..., None]

def fine_attention(fine_q, fine_k, fine_v, windows):
    group_size = HEADS_F // KV
    block_rows = math.gcd(TOKENS, 512)
    block_count = TOKENS // block_rows
    kv_width = KV * HEAD
    keys_padded = jnp.concatenate([jnp.zeros((WIN, kv_width), fine_k.dtype), fine_k], 0)
    values_padded = jnp.concatenate([jnp.zeros((WIN, kv_width), fine_v.dtype), fine_v], 0)

    def one_block(block_index):
        row_start = (block_index * block_rows).astype(jnp.int32)
        queries = lax.dynamic_slice_in_dim(fine_q, row_start, block_rows, 0).reshape(block_rows, KV, group_size, HEAD)
        key_rows = lax.dynamic_slice_in_dim(keys_padded, row_start, block_rows + WIN, 0).reshape(block_rows + WIN, KV, HEAD)
        value_rows = lax.dynamic_slice_in_dim(values_padded, row_start, block_rows + WIN, 0).reshape(block_rows + WIN, KV, HEAD)
        query_pos = row_start + jnp.arange(block_rows, dtype=jnp.int32)
        key_pos = row_start - WIN + jnp.arange(block_rows + WIN, dtype=jnp.int32)
        return attend_window(queries, key_rows, value_rows, query_pos, key_pos, windows)
    blocks = lax.map(one_block, jnp.arange(block_count, dtype=jnp.int32))
    return blocks.reshape(TOKENS, HEADS_F * HEAD)

def coarse_attention(queries, key_rows, value_rows):
    group_size = HEADS_C // KV
    query_heads = jnp.transpose(queries.reshape(COARSE, KV, group_size, HEAD), (1, 0, 2, 3))
    key_heads = jnp.transpose(key_rows.reshape(COARSE, KV, HEAD), (1, 0, 2))
    value_heads = jnp.transpose(value_rows.reshape(COARSE, KV, HEAD), (1, 0, 2))
    positions = jnp.arange(COARSE, dtype=jnp.int32)
    allowed = positions[None, :] <= positions[:, None]

    def one_group(operands):
        query_group, key_group, value_group = operands
        scores = jnp.einsum('qgd,ld->gql', query_group.astype(jnp.float32), key_group.astype(jnp.float32)) * HEAD ** (-0.5)
        scores = jnp.where(allowed[None], scores, -1e+30)
        row_top = scores.max(-1, keepdims=True)
        weights = jnp.where(allowed[None], jnp.exp(scores - row_top), 0.0)
        row_total = weights.sum(-1)
        mixed_heads = jnp.einsum('gql,ld->qgd', weights.astype(jnp.bfloat16).astype(jnp.float32), value_group.astype(jnp.float32))
        return mixed_heads / jnp.transpose(row_total, (1, 0))[..., None]
    result = lax.map(one_group, (query_heads, key_heads, value_heads))
    return jnp.transpose(result, (1, 0, 2, 3)).reshape(COARSE, HEADS_C * HEAD)

def reference(fine_x, fine_q, fine_k, fine_v, windows, pool_w, norm_gain, w_query, w_key, w_value, w_out, up_w):
    attended = fine_attention(fine_q, fine_k, fine_v, windows)
    stream = fine_x.astype(jnp.float32) + attended
    pooled_f = (stream.reshape(COARSE, POOL, D) * pool_w.astype(jnp.float32)[None]).sum(1)
    normed = (pooled_f * lax.rsqrt(lax.optimization_barrier(jnp.mean(pooled_f * pooled_f, -1, keepdims=True)) + 1e-05) * norm_gain.astype(jnp.float32)[None]).astype(jnp.bfloat16)
    queries = jnp.dot(normed, w_query, preferred_element_type=jnp.float32).astype(jnp.bfloat16)
    key_rows = jnp.dot(normed, w_key, preferred_element_type=jnp.float32).astype(jnp.bfloat16)
    value_rows = jnp.dot(normed, w_value, preferred_element_type=jnp.float32).astype(jnp.bfloat16)
    head_out = coarse_attention(queries, key_rows, value_rows).astype(jnp.bfloat16)
    coarse = pooled_f + jnp.dot(head_out, w_out, preferred_element_type=jnp.float32)
    shifted = jnp.concatenate([jnp.zeros((1, D), jnp.float32), coarse[:-1]], 0)
    result = stream.reshape(COARSE, POOL, D) + up_w.astype(jnp.float32)[None] * shifted[:, None, :]
    return result.reshape(TOKENS, D)
```

```python
import functools

import jax
import jax.numpy as jnp
from jax import lax
from jax.experimental import pallas as pl
from jax.experimental.pallas import tpu as pltpu
from jax.sharding import PartitionSpec as P

HEAD = 128
WIN = 512
POOL = 4
LOG2E = 1.4426950408889634
MESH = pl.DeviceIdType.MESH
F32 = jnp.float32
BF16 = jnp.bfloat16
VMEM_SPEC = pl.BlockSpec(memory_space=pltpu.VMEM)
ANY_SPEC = pl.BlockSpec(memory_space=pl.ANY)


def lanes(start, size):
    return pl.ds(pl.multiple_of(start, 128), size)


def fine_kernel(
    n_tp, n_dev, chunks, q_ref, k_ref, v_ref, x_ref, win_ref, pw_ref, gain_ref,
    stream_ref, pooled_ref, a_full, rs_full,
    kbuf, vbuf, dist, a_send, rs_send, ssq,
    hs_sem, hr_sem, as_sem, ar_sem, rss_sem, rsr_sem, loc_sem,
):
    rows = q_ref.shape[0]
    width = q_ref.shape[1]
    kv_width = k_ref.shape[1]
    reach = WIN // rows
    span = (reach + 1) * rows
    group = width // kv_width
    pool_rows = rows // POOL
    kv_chunk = kv_width // chunks
    q_chunk = width // chunks
    ctx = lax.axis_index("ctx")
    tp = lax.axis_index("tp")
    me = ctx * n_tp + tp

    def along(step):
        other = lax.rem(me + step + n_dev, n_dev)
        return (other // n_tp, lax.rem(other, n_tp))

    def peer(step):
        return (ctx, lax.rem(tp + step, n_tp))

    barrier = pltpu.get_barrier_semaphore()
    for d in range(1, reach + 1):
        pl.semaphore_signal(barrier, inc=1, device_id=along(-d), device_id_type=MESH)
    for d in range(1, n_tp):
        pl.semaphore_signal(barrier, inc=1, device_id=peer(d), device_id_type=MESH)
    pl.semaphore_wait(barrier, reach + n_tp - 1)

    def halo(hc, d, which):
        src, dst = ((k_ref, kbuf), (v_ref, vbuf))[which]
        cols = lanes(hc * kv_chunk, kv_chunk)
        return pltpu.make_async_remote_copy(
            src_ref=src.at[:, cols],
            dst_ref=dst.at[pl.ds((reach - d) * rows, rows), cols],
            send_sem=hs_sem.at[which, hc, d - 1],
            recv_sem=hr_sem.at[which, hc, d - 1],
            device_id=along(d),
            device_id_type=MESH,
        )

    for hc in range(chunks):
        for which in range(2):
            for d in range(1, reach + 1):
                halo(hc, d, which).start()

    kbuf[reach * rows :, :] = k_ref[...]
    vbuf[reach * rows :, :] = v_ref[...]
    q_at = lax.broadcasted_iota(jnp.int32, (rows, span), 0)
    l_at = lax.broadcasted_iota(jnp.int32, (rows, span), 1)
    gap = reach * rows + q_at - l_at
    outside = (gap < 0) | (l_at < (reach - me) * rows)
    dist[...] = jnp.where(outside, 2 * span, gap)
    ssq[...] = jnp.zeros_like(ssq)

    def a_copy(hc, step):
        cols = lanes(hc * q_chunk, q_chunk)
        return pltpu.make_async_remote_copy(
            src_ref=a_send.at[:, cols],
            dst_ref=a_full.at[tp, :, cols],
            send_sem=as_sem.at[hc, step],
            recv_sem=ar_sem.at[hc, tp],
            device_id=peer(step),
            device_id_type=MESH,
        )

    def a_arrival(hc, step):
        src_tp = lax.rem(tp + step, n_tp)
        cols = lanes(hc * q_chunk, q_chunk)
        return pltpu.make_async_remote_copy(
            src_ref=a_send.at[:, cols],
            dst_ref=a_full.at[src_tp, :, cols],
            send_sem=as_sem.at[hc, step],
            recv_sem=ar_sem.at[hc, src_tp],
            device_id=peer(step),
            device_id_type=MESH,
        )

    half = group // 2

    def chunk(hc, carry):
        for which in range(2):
            for d in range(1, reach + 1):
                halo(hc, d, which).wait_recv()
        for u in range(kv_chunk // HEAD):
            kv_cols = lanes(hc * kv_chunk + u * HEAD, HEAD)
            keys = kbuf[:, kv_cols]
            values = vbuf[:, kv_cols]
            for part in range(2):
                first = (hc * (kv_chunk // HEAD) + u) * group + part * half
                qs = jnp.concatenate(
                    [q_ref[:, lanes((first + i) * HEAD, HEAD)] for i in range(half)], axis=0
                )
                scores = lax.dot_general(
                    qs, keys, (((1,), (1,)), ((), ())), preferred_element_type=F32
                )
                weights, totals = [], []
                for i in range(half):
                    s = scores[i * rows : (i + 1) * rows] * (LOG2E * HEAD**-0.5)
                    s = jnp.where(dist[...] < win_ref[first + i], s, -1e30)
                    p = jnp.exp2(s - s.max(-1, keepdims=True))
                    totals.append(p.sum(-1, keepdims=True))
                    weights.append(p.astype(BF16))
                mixed = jnp.dot(
                    jnp.concatenate(weights, axis=0), values, preferred_element_type=F32
                )
                for i in range(half):
                    cols = lanes((first + i) * HEAD, HEAD)
                    stream_ref[first + i] = (
                        x_ref[:, cols].astype(F32) + mixed[i * rows : (i + 1) * rows] / totals[i]
                    )
        for i in range(q_chunk // HEAD):
            cols = lanes(hc * q_chunk + i * HEAD, HEAD)
            head = hc * (q_chunk // HEAD) + i
            pooled = sum(
                pw_ref[j : j + 1, cols] * stream_ref[head, pl.ds(j, pool_rows, stride=POOL), :]
                for j in range(POOL)
            )
            pooled_ref[:, cols] = pooled
            ssq[...] += pooled * pooled
            a_send[:, cols] = (pooled * gain_ref[:, cols]).astype(BF16)
        for step in range(1, n_tp):
            a_copy(hc, step).start()
        return carry

    lax.fori_loop(0, chunks, chunk, 0)

    mean = ssq[...].sum(-1, keepdims=True) * (1.0 / width)
    rs_send[...] = jnp.broadcast_to(lax.rsqrt(mean + 1e-05), rs_send.shape)

    def rs_copy(step):
        return pltpu.make_async_remote_copy(
            src_ref=rs_send,
            dst_ref=rs_full.at[tp],
            send_sem=rss_sem.at[step],
            recv_sem=rsr_sem.at[tp],
            device_id=peer(step),
            device_id_type=MESH,
        )

    def rs_arrival(step):
        src_tp = lax.rem(tp + step, n_tp)
        return pltpu.make_async_remote_copy(
            src_ref=rs_send,
            dst_ref=rs_full.at[src_tp],
            send_sem=rss_sem.at[step],
            recv_sem=rsr_sem.at[src_tp],
            device_id=peer(step),
            device_id_type=MESH,
        )

    for step in range(1, n_tp):
        rs_copy(step).start()
    own_a = pltpu.make_async_copy(a_send, a_full.at[tp], loc_sem.at[0])
    own_rs = pltpu.make_async_copy(rs_send, rs_full.at[tp], loc_sem.at[1])
    own_a.start()
    own_rs.start()
    own_a.wait()
    own_rs.wait()
    for hc in range(chunks):
        for which in range(2):
            for d in range(1, reach + 1):
                halo(hc, d, which).wait_send()
        for step in range(1, n_tp):
            a_copy(hc, step).wait_send()
            a_arrival(hc, step).wait_recv()
    for step in range(1, n_tp):
        rs_copy(step).wait_send()
        rs_arrival(step).wait_recv()


def fine_stage(mesh, fine_q, fine_k, fine_v, fine_x, windows, pool_w, gain):
    rows, width = fine_q.shape
    kv_width = fine_k.shape[1]
    n_tp = mesh.shape["tp"]
    n_dev = n_tp * mesh.shape["ctx"]
    chunks = 4
    reach = WIN // rows
    span = (reach + 1) * rows
    pool_rows = rows // POOL
    return pl.pallas_call(
        functools.partial(fine_kernel, n_tp, n_dev, chunks),
        out_shape=[
            jax.ShapeDtypeStruct((width // HEAD, rows, HEAD), F32),
            jax.ShapeDtypeStruct((pool_rows, width), F32),
            jax.ShapeDtypeStruct((n_tp, pool_rows, width), BF16),
            jax.ShapeDtypeStruct((n_tp, pool_rows, HEAD), F32),
        ],
        in_specs=[VMEM_SPEC] * 4 + [pl.BlockSpec(memory_space=pltpu.SMEM)] + [VMEM_SPEC] * 2,
        out_specs=[VMEM_SPEC, VMEM_SPEC, ANY_SPEC, ANY_SPEC],
        scratch_shapes=[
            pltpu.VMEM((span, kv_width), BF16),
            pltpu.VMEM((span, kv_width), BF16),
            pltpu.VMEM((rows, span), jnp.int32),
            pltpu.VMEM((pool_rows, width), BF16),
            pltpu.VMEM((pool_rows, HEAD), F32),
            pltpu.VMEM((pool_rows, HEAD), F32),
            pltpu.SemaphoreType.DMA((2, chunks, reach)),
            pltpu.SemaphoreType.DMA((2, chunks, reach)),
            pltpu.SemaphoreType.DMA((chunks, n_tp)),
            pltpu.SemaphoreType.DMA((chunks, n_tp)),
            pltpu.SemaphoreType.DMA((n_tp,)),
            pltpu.SemaphoreType.DMA((n_tp,)),
            pltpu.SemaphoreType.DMA((2,)),
        ],
        compiler_params=pltpu.CompilerParams(
            collective_id=0, has_side_effects=True, vmem_limit_bytes=40 * 2**20
        ),
        cost_estimate=pl.CostEstimate(
            flops=60_000_000_000, bytes_accessed=20 * 2**20, transcendentals=0
        ),
        name="fine_stage",
    )(fine_q, fine_k, fine_v, fine_x, windows, pool_w, gain)


def coarse_kernel(
    n_chip, a_hbm, rs_ref, w_hbm, out_ref,
    a_v, w_v, acc, kv_all, q_all, top, total, mixed,
    a_sem, w_sem, ds_sem, dr_sem, fs_sem, fr_sem,
):
    rows = a_v.shape[0]
    steps = a_sem.shape[0]
    depth = a_v.shape[1] // steps
    q_width = out_ref.shape[1]
    heads = q_width // HEAD
    ctx = lax.axis_index("ctx")
    tp = lax.axis_index("tp")
    chip = ctx // 2
    core = lax.rem(ctx, 2)
    sibling = chip * 2 + 1 - core

    barrier = pltpu.get_barrier_semaphore()
    for d in range(1, n_chip):
        other = lax.rem(chip + d, n_chip) * 2 + core
        pl.semaphore_signal(barrier, inc=1, device_id=(other, tp), device_id_type=MESH)
    pl.semaphore_signal(barrier, inc=1, device_id=(sibling, tp), device_id_type=MESH)

    def loads(k):
        return (
            pltpu.make_async_copy(
                a_hbm.at[:, lanes(k * depth, depth)], a_v.at[:, lanes(k * depth, depth)], a_sem.at[k]
            ),
            pltpu.make_async_copy(
                w_hbm.at[lanes(k * depth, depth)], w_v.at[lanes(k * depth, depth)], w_sem.at[k]
            ),
        )

    for k in range(steps):
        for load in loads(k):
            load.start()
    acc[...] = jnp.zeros_like(acc)

    def project(k, carry):
        for load in loads(k):
            load.wait()
        acc[...] += jnp.dot(
            a_v[:, lanes(k * depth, depth)],
            w_v[lanes(k * depth, depth), :],
            preferred_element_type=F32,
        )
        return carry

    lax.fori_loop(0, steps, project, 0)
    row_scale = rs_ref[:, 0:1]
    kv_all[ctx] = (acc[:, q_width:] * row_scale).astype(BF16)

    pl.semaphore_wait(barrier, n_chip)

    def direct(to_chip):
        return pltpu.make_async_remote_copy(
            src_ref=kv_all.at[ctx],
            dst_ref=kv_all.at[ctx],
            send_sem=ds_sem.at[to_chip],
            recv_sem=dr_sem.at[chip],
            device_id=(to_chip * 2 + core, tp),
            device_id_type=MESH,
        )

    def direct_arrival(from_chip):
        return pltpu.make_async_remote_copy(
            src_ref=kv_all.at[ctx],
            dst_ref=kv_all.at[from_chip * 2 + core],
            send_sem=ds_sem.at[from_chip],
            recv_sem=dr_sem.at[from_chip],
            device_id=(from_chip * 2 + core, tp),
            device_id_type=MESH,
        )

    def across(from_chip):
        return pltpu.make_async_remote_copy(
            src_ref=kv_all.at[from_chip * 2 + core],
            dst_ref=kv_all.at[from_chip * 2 + core],
            send_sem=fs_sem.at[from_chip],
            recv_sem=fr_sem.at[from_chip],
            device_id=(sibling, tp),
            device_id_type=MESH,
        )

    def across_arrival(from_chip):
        return pltpu.make_async_remote_copy(
            src_ref=kv_all.at[from_chip * 2 + core],
            dst_ref=kv_all.at[from_chip * 2 + 1 - core],
            send_sem=fs_sem.at[from_chip],
            recv_sem=fr_sem.at[from_chip],
            device_id=(sibling, tp),
            device_id_type=MESH,
        )

    def send(b, carry):
        direct(b).start()
        return carry

    across(chip).start()
    lax.fori_loop(chip + 1, n_chip, send, 0)

    for h in range(heads):
        q_all[h] = (acc[:, h * HEAD : (h + 1) * HEAD] * row_scale).astype(BF16)

    def attend(b, first):
        keys = jnp.concatenate([kv_all[2 * b, :, :HEAD], kv_all[2 * b + 1, :, :HEAD]], axis=0)
        values = jnp.concatenate([kv_all[2 * b, :, HEAD:], kv_all[2 * b + 1, :, HEAD:]], axis=0)
        for h in range(heads):
            s = lax.dot_general(
                q_all[h], keys, (((1,), (1,)), ((), ())), preferred_element_type=F32
            ) * (LOG2E * HEAD**-0.5)
            if first:
                q_at = core * rows + lax.broadcasted_iota(jnp.int32, s.shape, 0)
                k_at = lax.broadcasted_iota(jnp.int32, s.shape, 1)
                s = jnp.where(k_at <= q_at, s, -1e30)
                new_top = s.max(-1, keepdims=True)
                p = jnp.exp2(s - new_top)
                total[h] = p.sum(-1, keepdims=True)
                mixed[h] = jnp.dot(p.astype(BF16), values, preferred_element_type=F32)
            else:
                old = top[h]
                new_top = jnp.maximum(old, s.max(-1, keepdims=True))
                keep = jnp.exp2(old - new_top)
                p = jnp.exp2(s - new_top)
                total[h] = total[h] * keep + p.sum(-1, keepdims=True)
                mixed[h] = mixed[h] * keep + jnp.dot(
                    p.astype(BF16), values, preferred_element_type=F32
                )
            top[h] = new_top

    across_arrival(chip).wait_recv()
    attend(chip, True)

    def forward(b, carry):
        direct_arrival(b).wait_recv()
        across(b).start()
        return carry

    lax.fori_loop(0, chip, forward, 0)

    def earlier(b, carry):
        across_arrival(b).wait_recv()
        attend(b, False)
        return carry

    lax.fori_loop(0, chip, earlier, 0)
    for h in range(heads):
        out_ref[:, h * HEAD : (h + 1) * HEAD] = (mixed[h] / total[h]).astype(BF16)

    def drain_direct(b, carry):
        direct(b).wait_send()
        return carry

    def drain_across(b, carry):
        across(b).wait_send()
        return carry

    lax.fori_loop(chip + 1, n_chip, drain_direct, 0)
    lax.fori_loop(0, chip + 1, drain_across, 0)


def coarse_stage(mesh, a_full, rs_full, w_full, q_width):
    rows, width = a_full.shape
    n_ctx = mesh.shape["ctx"]
    steps = 16
    kv2 = w_full.shape[1] - q_width
    heads = q_width // HEAD
    return pl.pallas_call(
        functools.partial(coarse_kernel, n_ctx // 2),
        out_shape=jax.ShapeDtypeStruct((rows, q_width), BF16),
        in_specs=[ANY_SPEC, VMEM_SPEC, ANY_SPEC],
        out_specs=VMEM_SPEC,
        scratch_shapes=[
            pltpu.VMEM((rows, width), BF16),
            pltpu.VMEM(w_full.shape, BF16),
            pltpu.VMEM((rows, w_full.shape[1]), F32),
            pltpu.VMEM((n_ctx, rows, kv2), BF16),
            pltpu.VMEM((heads, rows, HEAD), BF16),
            pltpu.VMEM((heads, rows, 1), F32),
            pltpu.VMEM((heads, rows, 1), F32),
            pltpu.VMEM((heads, rows, HEAD), F32),
            pltpu.SemaphoreType.DMA((steps,)),
            pltpu.SemaphoreType.DMA((steps,)),
            pltpu.SemaphoreType.DMA((n_ctx // 2,)),
            pltpu.SemaphoreType.DMA((n_ctx // 2,)),
            pltpu.SemaphoreType.DMA((n_ctx // 2,)),
            pltpu.SemaphoreType.DMA((n_ctx // 2,)),
        ],
        compiler_params=pltpu.CompilerParams(
            collective_id=1, has_side_effects=True, vmem_limit_bytes=40 * 2**20
        ),
        cost_estimate=pl.CostEstimate(
            flops=40_000_000_000, bytes_accessed=20 * 2**20, transcendentals=0
        ),
        name="coarse_stage",
    )(a_full, rs_full, w_full)


def out_kernel(
    n_tp, n_dev, heads_ref, pooled_ref, w_hbm, shifted_ref,
    w_v, sent, got, coarse, last_send, last_got,
    w_sem, s_sem, r_sem, l_sem,
):
    rows = heads_ref.shape[0]
    own = pooled_ref.shape[0]
    blocks, depth, cols = w_v.shape
    groups = s_sem.shape[0]
    per = blocks // groups
    ctx = lax.axis_index("ctx")
    tp = lax.axis_index("tp")
    me = ctx * n_tp + tp

    def along(step):
        other = lax.rem(me + step + n_dev, n_dev)
        return (other // n_tp, lax.rem(other, n_tp))

    def peer(step):
        return (ctx, lax.rem(tp + step, n_tp))

    barrier = pltpu.get_barrier_semaphore()
    for d in range(1, n_tp):
        pl.semaphore_signal(barrier, inc=1, device_id=peer(d), device_id_type=MESH)
    pl.semaphore_signal(barrier, inc=1, device_id=along(-1), device_id_type=MESH)

    def load(b):
        return pltpu.make_async_copy(w_hbm.at[b], w_v.at[b], w_sem.at[b])

    for b in range(blocks):
        load(b).start()

    pl.semaphore_wait(barrier, n_tp)

    def partial_copy(g, step):
        to = lax.rem(tp + step, n_tp)
        where = lanes(g * per * cols, per * cols)
        return pltpu.make_async_remote_copy(
            src_ref=sent.at[to, :, where],
            dst_ref=got.at[tp, :, where],
            send_sem=s_sem.at[g, step],
            recv_sem=r_sem.at[g, tp],
            device_id=peer(step),
            device_id_type=MESH,
        )

    def partial_arrival(g, step):
        source = lax.rem(tp + step, n_tp)
        where = lanes(g * per * cols, per * cols)
        return pltpu.make_async_remote_copy(
            src_ref=sent.at[source, :, where],
            dst_ref=got.at[source, :, where],
            send_sem=s_sem.at[g, step],
            recv_sem=r_sem.at[g, source],
            device_id=peer(step),
            device_id_type=MESH,
        )

    def multiply(g, carry):
        for i in range(per):
            b = g * per + i
            load(b).wait()
            product = jnp.dot(heads_ref[...], w_v[b], preferred_element_type=F32).astype(BF16)
            for p in range(n_tp):
                sent[p, :, lanes(b * cols, cols)] = product[p * own : (p + 1) * own]
        for step in range(1, n_tp):
            partial_copy(g, step).start()
        return carry

    lax.fori_loop(0, groups, multiply, 0)

    def gather(g, carry):
        where = lanes(g * per * cols, per * cols)
        for step in range(1, n_tp):
            partial_arrival(g, step).wait_recv()
        value = pooled_ref[:, where] + sent[tp, :, where].astype(F32)
        for step in range(1, n_tp):
            value += got[lax.rem(tp + step, n_tp), :, where].astype(F32)
        coarse[:, where] = value
        return carry

    lax.fori_loop(0, groups, gather, 0)

    piece = last_send.shape[1]
    for i in range(last_send.shape[0]):
        last_send[i : i + 1, :] = coarse[own - 1 : own, i * piece : (i + 1) * piece]
    last = pltpu.make_async_remote_copy(
        src_ref=last_send,
        dst_ref=last_got,
        send_sem=l_sem.at[0],
        recv_sem=l_sem.at[1],
        device_id=along(1),
        device_id_type=MESH,
    )
    last.start()
    shifted_ref[1:own, :] = coarse[0 : own - 1, :]
    last.wait()
    first_row = jnp.where(me == 0, 0.0, last_got[...])
    for i in range(last_send.shape[0]):
        shifted_ref[0:1, i * piece : (i + 1) * piece] = first_row[i : i + 1, :]

    def drain(g, carry):
        for step in range(1, n_tp):
            partial_copy(g, step).wait_send()
        return carry

    lax.fori_loop(0, groups, drain, 0)


def out_stage(mesh, heads, pooled, w_full):
    own, width = pooled.shape
    n_tp = mesh.shape["tp"]
    n_dev = n_tp * mesh.shape["ctx"]
    groups = 8
    blocks = w_full.shape[0]
    return pl.pallas_call(
        functools.partial(out_kernel, n_tp, n_dev),
        out_shape=jax.ShapeDtypeStruct((own, width), F32),
        in_specs=[VMEM_SPEC, VMEM_SPEC, ANY_SPEC],
        out_specs=VMEM_SPEC,
        scratch_shapes=[
            pltpu.VMEM(w_full.shape, BF16),
            pltpu.VMEM((n_tp, own, width), BF16),
            pltpu.VMEM((n_tp, own, width), BF16),
            pltpu.VMEM((own, width), F32),
            pltpu.VMEM((8, width // 8), F32),
            pltpu.VMEM((8, width // 8), F32),
            pltpu.SemaphoreType.DMA((blocks,)),
            pltpu.SemaphoreType.DMA((groups, n_tp)),
            pltpu.SemaphoreType.DMA((groups, n_tp)),
            pltpu.SemaphoreType.DMA((2,)),
        ],
        compiler_params=pltpu.CompilerParams(
            collective_id=2, has_side_effects=True, vmem_limit_bytes=40 * 2**20
        ),
        cost_estimate=pl.CostEstimate(
            flops=40_000_000_000, bytes_accessed=20 * 2**20, transcendentals=0
        ),
        name="out_stage",
    )(heads, pooled, w_full)


def combine_kernel(stream_ref, shifted_ref, up_ref, out_ref, spread):
    pool_rows = shifted_ref.shape[0]
    for i in range(stream_ref.shape[0]):
        cols = slice(i * HEAD, (i + 1) * HEAD)
        shifted = shifted_ref[:, cols]
        for j in range(POOL):
            spread[i, pl.ds(j, pool_rows, stride=POOL), :] = up_ref[j : j + 1, cols] * shifted
        out_ref[:, cols] = stream_ref[i] + spread[i]


def combine_stage(stream, shifted, up_w):
    n_heads, rows, _ = stream.shape
    width = n_heads * HEAD
    block = 1024
    per = block // HEAD
    return pl.pallas_call(
        combine_kernel,
        out_shape=jax.ShapeDtypeStruct((rows, width), F32),
        grid=(width // block,),
        in_specs=[
            pl.BlockSpec((per, rows, HEAD), lambda i: (i, 0, 0)),
            pl.BlockSpec((shifted.shape[0], block), lambda i: (0, i)),
            pl.BlockSpec((up_w.shape[0], block), lambda i: (0, i)),
        ],
        out_specs=pl.BlockSpec((rows, block), lambda i: (0, i)),
        scratch_shapes=[pltpu.VMEM((per, rows, HEAD), F32)],
        name="combine_stage",
    )(stream, shifted, up_w)


def per_device(
    mesh, fine_x, fine_q, fine_k, fine_v, windows, pool_w, norm_gain, w_query, w_key, w_value, w_out, up_w
):
    w_local = jnp.concatenate([w_query, w_key, w_value], axis=1)
    w_full = lax.all_gather(w_local, "ctx", axis=0, tiled=True)
    out_full = lax.all_gather(w_out, "ctx", axis=0, tiled=False)
    stream, pooled, a_full, rs_full = fine_stage(
        mesh, fine_q, fine_k, fine_v, fine_x, windows, pool_w, norm_gain[None]
    )
    a_rows = a_full.reshape(-1, a_full.shape[-1])
    rs_rows = rs_full.reshape(-1, rs_full.shape[-1])
    heads = coarse_stage(mesh, a_rows, rs_rows, w_full, w_query.shape[1])
    shifted = out_stage(mesh, heads, pooled, out_full)
    return combine_stage(stream, shifted, up_w)


def solution(mesh):
    placed = (
        P(("ctx", "tp"), None),
        P(("ctx", "tp"), None),
        P(("ctx", "tp"), None),
        P(("ctx", "tp"), None),
        P(),
        P(),
        P(),
        P("ctx", "tp"),
        P("ctx", "tp"),
        P("ctx", "tp"),
        P("tp", "ctx"),
        P(),
    )
    return jax.shard_map(
        functools.partial(per_device, mesh),
        mesh=mesh,
        in_specs=placed,
        out_specs=P(("ctx", "tp"), None),
        check_vma=False,
    )
```

```python
import functools

import jax
import jax.numpy as jnp
from jax import lax
from jax.experimental import pallas as pl
from jax.experimental.pallas import tpu as pltpu
from jax.sharding import PartitionSpec as P

HEAD = 128
WIN = 512
POOL = 4
RING = 4
LOG2E = 1.4426950408889634
MESH = pl.DeviceIdType.MESH
F32 = jnp.float32
BF16 = jnp.bfloat16
VMEM_SPEC = pl.BlockSpec(memory_space=pltpu.VMEM)
ANY_SPEC = pl.BlockSpec(memory_space=pl.ANY)
CHUNKS = 4
GROUPS = 8


def lanes(start, size):
    return pl.ds(pl.multiple_of(start, 128), size)


def sublanes(start, size):
    return pl.ds(pl.multiple_of(start, size), size)


def block_kernel(
    q_ref, k_ref, v_ref, x_ref, win_ref, pw_ref, gain_ref, up_ref, wq_hbm, wk_hbm, wv_hbm, wo_hbm,
    out_hbm,
    kbuf, vbuf, dist, stream, pooled_v, a_full, rs_all, ssq,
    w_all, wo_all, acc, kv_all, q_all, top, total, mixed, heads_v,
    keep, s_send, s_got, y_send, y_got, shifted, last_send, last_got,
    hs_sem, hr_sem, as_sem, ar_sem, af_sem, rss_sem, rsr_sem,
    ho_sem, wgs_sem, wgr_sem, kvs_sem, kvr_sem,
    ss_sem, sr_sem, ys_sem, yr_sem, l_sem, o_sem,
):
    rows, width = q_ref.shape
    kv_width = k_ref.shape[1]
    reach = WIN // rows
    span = (reach + 1) * rows
    group = width // kv_width
    own = rows // POOL
    kv_chunk = kv_width // CHUNKS
    q_chunk = width // CHUNKS
    n_ctx = w_all.shape[0]
    depth = w_all.shape[1]
    half = depth // 2
    q_width = heads_v.shape[1]
    heads = q_width // HEAD
    all_rows = heads_v.shape[0]
    n_tp = 2 * RING
    n_dev = n_ctx * n_tp

    ctx = lax.axis_index("ctx")
    tp = lax.axis_index("tp")
    me = ctx * n_tp + tp
    x_lo = ctx // n_tp
    z = lax.rem(ctx, n_tp) // 2
    core = lax.rem(ctx, 2)
    x_hi = tp // RING
    y = lax.rem(tp, RING)
    x = 2 * x_hi + x_lo
    pair = x_lo * RING + z
    mine = pair * 2 + x_hi
    slot = core * RING + y

    def at(x_at, z_at, y_at, core_at):
        return (lax.rem(x_at, 2) * n_tp + z_at * 2 + core_at, (x_at // 2) * RING + y_at)

    def along(step):
        other = lax.rem(me + step + n_dev, n_dev)
        return (other // n_tp, lax.rem(other, n_tp))

    def turn(value, step):
        return lax.rem(value + step + 2 * RING, RING)

    def y_dev(step):
        return at(x, z, turn(y, step), core)

    def group_dev(g):
        p = g // 2
        return at(2 * lax.rem(g, 2) + p // RING, lax.rem(p, RING), y, core)

    sibling = at(x, z, y, 1 - core)

    def remote(src, dst, send_sem, recv_sem, device):
        return pltpu.make_async_remote_copy(
            src_ref=src, dst_ref=dst, send_sem=send_sem, recv_sem=recv_sem,
            device_id=device, device_id_type=MESH,
        )

    barrier = pltpu.get_barrier_semaphore()

    def greet(device):
        pl.semaphore_signal(barrier, inc=1, device_id=device, device_id_type=MESH)

    for e in range(1, RING):
        greet(y_dev(e))
        greet(at(x, z, turn(y, e), 1 - core))
    greet(sibling)
    greet(along(-reach))
    greet(along(-1))

    def greet_plane(d, carry):
        greet(group_dev(lax.rem(mine + d, n_ctx)))
        return carry

    lax.fori_loop(1, n_ctx, greet_plane, 0)
    pl.semaphore_wait(barrier, 2 * RING + 1 + n_ctx - 1)

    def block_cols(hc):
        return lanes(hc * kv_chunk, kv_chunk)

    def halo_copy(which, hc, d, device, source):
        buf = (kbuf, vbuf)[which]
        return remote(
            buf.at[sublanes(source * rows, rows), block_cols(hc)],
            buf.at[pl.ds((reach - d) * rows, rows), block_cols(hc)],
            hs_sem.at[which, hc, d - 1],
            hr_sem.at[which, hc, d - 1],
            device,
        )

    def halo_far(which, hc):
        return halo_copy(which, hc, reach, along(reach), reach)

    def halo_near(which, hc, e):
        return halo_copy(which, hc, e, y_dev(e), jnp.where(y + e < RING, reach, 0))

    kbuf[reach * rows :, :] = k_ref[...]
    vbuf[reach * rows :, :] = v_ref[...]
    for hc in range(CHUNKS):
        for which in range(2):
            halo_far(which, hc).start()

    is_home = core == x_hi

    def shard_parts(to):
        return (
            (wq_hbm, w_all.at[to, :, 0:q_width]),
            (wk_hbm, w_all.at[to, :, q_width : q_width + HEAD]),
            (wv_hbm, w_all.at[to, :, q_width + HEAD : q_width + 2 * HEAD]),
            (wo_hbm, wo_all.at[to]),
        )

    def hand_over(i):
        src, dst = shard_parts(ctx)[i]
        return remote(src, dst, ho_sem.at[0, i], ho_sem.at[1, i], sibling)

    def hand_over_arrival(i):
        src, dst = shard_parts(ctx + 1 - 2 * core)[i]
        return remote(src, dst, ho_sem.at[0, i], ho_sem.at[1, i], sibling)

    def stay(i):
        src, dst = shard_parts(ctx)[i]
        return pltpu.make_async_copy(src, dst, ho_sem.at[2, i])

    @pl.when(is_home)
    def _():
        for i in range(4):
            stay(i).start()

    @pl.when(jnp.logical_not(is_home))
    def _():
        for i in range(4):
            hand_over(i).start()

    for hc in range(CHUNKS):
        for which in range(2):
            for e in range(1, RING):

                @pl.when(y + e < RING)
                def _():
                    halo_near(which, hc, e).start()

    def offsets(src):
        off_x = turn(x, -2 * core - src // n_tp)
        off_z = turn(z, -(lax.rem(src, n_tp) // 2))
        return off_x, off_z, lax.rem(src, 2)

    def hop(kind, path, src, lane):
        buf = (w_all, wo_all)[kind]
        piece = buf.at[src, pl.ds(path * half, half), :]
        device = (
            at(turn(x, 1), z, y, core),
            at(turn(x, -1), z, y, core),
            at(x, turn(z, 1), y, core),
            at(x, turn(z, -1), y, core),
        )[lane]
        return remote(
            piece, piece, wgs_sem.at[kind, path, src, lane], wgr_sem.at[kind, path, src], device
        )

    def hop_wanted(path, src, lane):
        off_x, off_z, c = offsets(src)
        off = off_x if lane < 2 else off_z
        if lane % 2 == 0:
            wanted = (off == 0) | ((off == 1) & (c == 0))
        else:
            wanted = (off == 0) | ((off == 3) & (c == 1))
        if path == 0 and lane < 2:
            wanted = wanted & (off_z == 0)
        if path == 1 and lane >= 2:
            wanted = wanted & (off_x == 0)
        return wanted

    def launch(kind, path, src):
        for lane in range(4):

            @pl.when(hop_wanted(path, src, lane))
            def _():
                hop(kind, path, src, lane).start()

    def arrive(kind, path, src):
        hop(kind, path, src, 0).wait_recv()
        launch(kind, path, src)

    def settle(kind):
        def one(src, carry):
            for path in range(2):
                for lane in range(4):

                    @pl.when(hop_wanted(path, src, lane))
                    def _():
                        hop(kind, path, src, lane).wait_send()

            return carry

        lax.fori_loop(0, n_ctx, one, 0)

    def origin(kind):
        @pl.when(is_home)
        def _():
            for i in range(4):
                if (i == 3) == (kind == 1):
                    stay(i).wait()
                    hand_over_arrival(i).wait_recv()
            for c in range(2):
                src = x_lo * n_tp + z * 2 + c
                launch(kind, 0, src)
                launch(kind, 1, src)

    def first_phase(kind):
        def one(i, carry):
            j, c = i // 2, lax.rem(i, 2)
            src = j * n_tp + z * 2 + c
            off_x, _, _ = offsets(src)

            @pl.when(off_x != 0)
            def _():
                arrive(kind, 0, src)

            return carry

        def two(i, carry):
            order, c = i // 2, lax.rem(i, 2)
            off = jnp.where(order == 0, 1, RING - order)
            arrive(kind, 1, x_lo * n_tp + turn(z, -off) * 2 + c)
            return carry

        lax.fori_loop(0, 4, one, 0)

        @pl.when(is_home)
        def _():
            lax.fori_loop(0, 6, two, 0)

    def second_phase(kind, step):
        off_first = jnp.where(step == 0, 1, RING - step)
        off_second = jnp.where(step < 2, step, 5 - step)

        def one(i, carry):
            j, c = i // 2, lax.rem(i, 2)

            @pl.when(step < 3)
            def _():
                arrive(kind, 0, j * n_tp + turn(z, -off_first) * 2 + c)

            src = j * n_tp + turn(z, -off_second) * 2 + c
            off_x, _, _ = offsets(src)

            @pl.when(off_x != 0)
            def _():
                arrive(kind, 1, src)

            return carry

        lax.fori_loop(0, 4, one, 0)

    origin(0)

    for hc in range(CHUNKS):
        for which in range(2):
            halo_far(which, hc).wait_recv()
        for which in range(2):
            for e in range(1, RING):

                @pl.when(y + e >= RING)
                def _():
                    halo_near(which, hc, e).start()

    q_at = lax.broadcasted_iota(jnp.int32, (rows, span), 0)
    l_at = lax.broadcasted_iota(jnp.int32, (rows, span), 1)
    gap = reach * rows + q_at - l_at
    outside = (gap < 0) | (l_at < (reach - me) * rows)
    dist[...] = jnp.where(outside, 2 * span, gap)
    ssq[...] = jnp.zeros_like(ssq)

    def a_rows(s):
        return sublanes(s * own, own)

    def a_piece(hc, s):
        return a_full.at[a_rows(s), lanes(hc * q_chunk, q_chunk)]

    def a_copy(hc, e):
        piece = a_piece(hc, slot)
        device = sibling if e == 0 else y_dev(e)
        return remote(piece, piece, as_sem.at[hc, e], ar_sem.at[hc, slot], device)

    def a_onward(hc, e):
        s = core * RING + turn(y, -e)
        piece = a_piece(hc, s)
        return remote(piece, piece, af_sem.at[hc, e], ar_sem.at[hc, s], sibling)

    def a_other(hc, y_at):
        s = (1 - core) * RING + y_at
        piece = a_piece(hc, s)
        return remote(piece, piece, af_sem.at[hc, 0], ar_sem.at[hc, s], sibling)

    part_heads = group // 2

    def chunk(hc, carry):
        for which in range(2):
            for e in range(1, RING):
                halo_near(which, hc, e).wait_recv()
        for u in range(kv_chunk // HEAD):
            kv_cols = lanes(hc * kv_chunk + u * HEAD, HEAD)
            keys = kbuf[:, kv_cols]
            values = vbuf[:, kv_cols]
            for part in range(2):
                first = (hc * (kv_chunk // HEAD) + u) * group + part * part_heads
                qs = jnp.concatenate(
                    [q_ref[:, lanes((first + i) * HEAD, HEAD)] for i in range(part_heads)], axis=0
                )
                scores = lax.dot_general(
                    qs, keys, (((1,), (1,)), ((), ())), preferred_element_type=F32
                )
                weights, totals = [], []
                for i in range(part_heads):
                    s = scores[i * rows : (i + 1) * rows] * (LOG2E * HEAD**-0.5)
                    s = jnp.where(dist[...] < win_ref[first + i], s, -1e30)
                    p = jnp.exp2(s - s.max(-1, keepdims=True))
                    totals.append(p.sum(-1, keepdims=True))
                    weights.append(p.astype(BF16))
                out = jnp.dot(
                    jnp.concatenate(weights, axis=0), values, preferred_element_type=F32
                )
                for i in range(part_heads):
                    cols = lanes((first + i) * HEAD, HEAD)
                    stream[first + i] = (
                        x_ref[:, cols].astype(F32) + out[i * rows : (i + 1) * rows] / totals[i]
                    )
        for i in range(q_chunk // HEAD):
            cols = lanes(hc * q_chunk + i * HEAD, HEAD)
            head = hc * (q_chunk // HEAD) + i
            pooled = sum(
                pw_ref[j : j + 1, cols] * stream[head, pl.ds(j, own, stride=POOL), :]
                for j in range(POOL)
            )
            pooled_v[:, cols] = pooled
            ssq[...] += pooled * pooled
            a_full[a_rows(slot), cols] = (pooled * gain_ref[:, cols]).astype(BF16)
        for e in range(RING):
            a_copy(hc, e).start()

        @pl.when(hc == 0)
        def _():
            first_phase(0)

        @pl.when(hc > 0)
        def _():
            second_phase(0, hc - 1)

        return carry

    lax.fori_loop(0, CHUNKS, chunk, 0)

    mean = ssq[...].sum(-1, keepdims=True) * (1.0 / width)
    rs_all[slot] = jnp.broadcast_to(lax.rsqrt(mean + 1e-05), ssq.shape)

    def rs_copy(e, other):
        device = at(x, z, turn(y, e), 1 - core if other else core)
        return remote(
            rs_all.at[slot], rs_all.at[slot], rss_sem.at[other, e], rsr_sem.at[slot], device
        )

    def rs_arrival(e, other):
        s = (1 - core if other else core) * RING + turn(y, e)
        return remote(
            rs_all.at[s], rs_all.at[s], rss_sem.at[other, e], rsr_sem.at[s], sibling
        )

    others = [(e, other) for other in range(2) for e in range(RING) if (e, other) != (0, 0)]
    for e, other in others:
        rs_copy(e, other).start()

    def a_relay(hc, carry):
        for e in range(1, RING):
            a_onward(hc, e).wait_recv()
            a_onward(hc, e).start()
        return carry

    lax.fori_loop(0, CHUNKS, a_relay, 0)
    second_phase(0, jnp.int32(3))

    def a_finish(hc, carry):
        for y_at in range(RING):
            a_other(hc, y_at).wait_recv()
        return carry

    lax.fori_loop(0, CHUNKS, a_finish, 0)
    for e, other in others:
        rs_arrival(e, other).wait_recv()
    origin(1)

    acc[...] = jnp.zeros_like(acc)

    def project(k, carry):
        acc[...] += jnp.dot(
            a_full[:, lanes(k * depth, depth)], w_all[k], preferred_element_type=F32
        )
        return carry

    lax.fori_loop(0, n_ctx, project, 0)
    row_scale = jnp.concatenate([rs_all[s] for s in range(n_tp)], axis=0)[:, 0:1]
    kv_all[mine] = (acc[:, q_width:] * row_scale).astype(BF16)

    def kv_copy(to):
        return remote(
            kv_all.at[mine], kv_all.at[mine], kvs_sem.at[to], kvr_sem.at[mine], group_dev(to)
        )

    def kv_arrival(source):
        return remote(
            kv_all.at[source], kv_all.at[source], kvs_sem.at[source], kvr_sem.at[source],
            group_dev(source),
        )

    partner = pair * 2 + 1 - x_hi

    def kv_send(to, carry):
        kv_copy(to).start()
        return carry

    kv_copy(partner).start()
    lax.fori_loop(pair * 2 + 2, n_ctx, kv_send, 0)
    for h in range(heads):
        q_all[h] = (acc[:, h * HEAD : (h + 1) * HEAD] * row_scale).astype(BF16)

    def attend(b, first):
        keys = jnp.concatenate([kv_all[2 * b, :, :HEAD], kv_all[2 * b + 1, :, :HEAD]], axis=0)
        values = jnp.concatenate([kv_all[2 * b, :, HEAD:], kv_all[2 * b + 1, :, HEAD:]], axis=0)
        for h in range(heads):
            s = lax.dot_general(
                q_all[h], keys, (((1,), (1,)), ((), ())), preferred_element_type=F32
            ) * (LOG2E * HEAD**-0.5)
            if first:
                run = all_rows // 2
                row = lax.broadcasted_iota(jnp.int32, s.shape, 0)
                col = lax.broadcasted_iota(jnp.int32, s.shape, 1)
                q_pos = row + x_hi * run + jnp.where(row >= run, run, 0)
                in_block = jnp.where(col >= all_rows, col - all_rows, col)
                k_pos = (
                    in_block + jnp.where(col >= all_rows, run, 0) + jnp.where(in_block >= run, run, 0)
                )
                s = jnp.where(k_pos <= q_pos, s, -1e30)
                new_top = s.max(-1, keepdims=True)
                p = jnp.exp2(s - new_top)
                total[h] = p.sum(-1, keepdims=True)
                mixed[h] = jnp.dot(p.astype(BF16), values, preferred_element_type=F32)
            else:
                old = top[h]
                new_top = jnp.maximum(old, s.max(-1, keepdims=True))
                scale = jnp.exp2(old - new_top)
                p = jnp.exp2(s - new_top)
                total[h] = total[h] * scale + p.sum(-1, keepdims=True)
                mixed[h] = mixed[h] * scale + jnp.dot(
                    p.astype(BF16), values, preferred_element_type=F32
                )
            top[h] = new_top

    kv_arrival(partner).wait_recv()
    attend(pair, True)

    def earlier(b, carry):
        @pl.when(b < pair)
        def _():
            kv_arrival(2 * b).wait_recv()
            kv_arrival(2 * b + 1).wait_recv()
            attend(b, False)

        @pl.when(b == 1)
        def _():
            first_phase(1)

        @pl.when((b >= 3) & (b < 7))
        def _():
            second_phase(1, b - 3)

        return carry

    lax.fori_loop(0, n_ctx // 2, earlier, 0)
    for h in range(heads):
        heads_v[:, h * HEAD : (h + 1) * HEAD] = (mixed[h] / total[h]).astype(BF16)

    per = n_ctx // GROUPS
    cols_out = wo_all.shape[2]
    wide = per * cols_out

    def s_copy(g):
        where = lanes(g * wide, wide)
        return remote(s_send.at[:, where], s_got.at[:, where], ss_sem.at[g], sr_sem.at[g], sibling)

    def multiply(g, carry):
        for i in range(per):
            b = g * per + i
            where = lanes(b * cols_out, cols_out)
            product = jnp.dot(heads_v[...], wo_all[b], preferred_element_type=F32)
            low, high = product[: all_rows // 2], product[all_rows // 2 :]
            keep[:, where] = jnp.where(core == 0, low, high).astype(BF16)
            s_send[:, where] = jnp.where(core == 0, high, low).astype(BF16)
        s_copy(g).start()
        return carry

    lax.fori_loop(0, GROUPS, multiply, 0)

    def y_copy(g, e):
        where = lanes(g * wide, wide)
        return remote(
            y_send.at[a_rows(turn(y, e)), where], y_got.at[a_rows(y), where],
            ys_sem.at[g, e], yr_sem.at[g, y], y_dev(e),
        )

    def y_arrival(g, e):
        where = lanes(g * wide, wide)
        source = turn(y, e)
        return remote(
            y_send.at[a_rows(source), where], y_got.at[a_rows(source), where],
            ys_sem.at[g, e], yr_sem.at[g, source], y_dev(e),
        )

    def reduce_cores(g, carry):
        where = lanes(g * wide, wide)
        s_copy(g).wait_recv()
        y_send[:, where] = (keep[:, where].astype(F32) + s_got[:, where].astype(F32)).astype(BF16)
        for e in range(1, RING):
            y_copy(g, e).start()
        pooled_v[:, where] += (
            keep[a_rows(y), where].astype(F32) + s_got[a_rows(y), where].astype(F32)
        )
        return carry

    lax.fori_loop(0, GROUPS, reduce_cores, 0)

    def reduce_ring(g, carry):
        where = lanes(g * wide, wide)
        for e in range(1, RING):
            y_arrival(g, e).wait_recv()
        value = pooled_v[:, where]
        for e in range(1, RING):
            value += y_got[a_rows(turn(y, e)), where].astype(F32)
        pooled_v[:, where] = value
        return carry

    lax.fori_loop(0, GROUPS, reduce_ring, 0)

    piece = last_send.shape[1]
    for i in range(last_send.shape[0]):
        last_send[i : i + 1, :] = pooled_v[own - 1 : own, i * piece : (i + 1) * piece]
    last = remote(last_send, last_got, l_sem.at[0], l_sem.at[1], along(1))
    last.start()
    shifted[1:own, :] = pooled_v[0 : own - 1, :]
    last.wait()
    first_row = jnp.where(me == 0, 0.0, last_got[...])
    for i in range(last_send.shape[0]):
        shifted[0:1, i * piece : (i + 1) * piece] = first_row[i : i + 1, :]

    def result(h):
        return pltpu.make_async_copy(
            stream.at[h], out_hbm.at[:, lanes(h * HEAD, HEAD)], o_sem.at[h]
        )

    def combine(i, carry):
        for u in range(group):
            h = i * group + u
            cols = lanes(h * HEAD, HEAD)
            add = shifted[:, cols]
            for j in range(POOL):
                where = pl.ds(j, own, stride=POOL)
                stream[h, where, :] = stream[h, where, :] + up_ref[j : j + 1, cols] * add
            result(h).start()
        return carry

    lax.fori_loop(0, width // HEAD // group, combine, 0)

    for hc in range(CHUNKS):
        for which in range(2):
            halo_far(which, hc).wait_send()
            for e in range(1, RING):
                halo_near(which, hc, e).wait_send()

    @pl.when(jnp.logical_not(is_home))
    def _():
        for i in range(4):
            hand_over(i).wait_send()

    settle(0)
    settle(1)

    def a_settle(hc, carry):
        for e in range(RING):
            a_copy(hc, e).wait_send()
        for e in range(1, RING):
            a_onward(hc, e).wait_send()
        return carry

    lax.fori_loop(0, CHUNKS, a_settle, 0)
    for e, other in others:
        rs_copy(e, other).wait_send()

    def kv_settle(to, carry):
        kv_copy(to).wait_send()
        return carry

    kv_copy(partner).wait_send()
    lax.fori_loop(pair * 2 + 2, n_ctx, kv_settle, 0)

    def sums_settle(g, carry):
        s_copy(g).wait_send()
        for e in range(1, RING):
            y_copy(g, e).wait_send()
        return carry

    lax.fori_loop(0, GROUPS, sums_settle, 0)

    def out_settle(h, carry):
        result(h).wait()
        return carry

    lax.fori_loop(0, width // HEAD, out_settle, 0)


def per_device(
    mesh, fine_x, fine_q, fine_k, fine_v, windows, pool_w, norm_gain, w_query, w_key, w_value, w_out, up_w
):
    rows, width = fine_q.shape
    kv_width = fine_k.shape[1]
    n_tp, n_ctx = mesh.shape["tp"], mesh.shape["ctx"]
    reach = WIN // rows
    span = (reach + 1) * rows
    own = rows // POOL
    all_rows = own * n_tp
    depth, q_width = w_query.shape
    heads = q_width // HEAD
    w_cols = q_width + 2 * HEAD
    dma = pltpu.SemaphoreType.DMA
    return pl.pallas_call(
        block_kernel,
        out_shape=jax.ShapeDtypeStruct((rows, width), F32),
        in_specs=[VMEM_SPEC] * 4
        + [pl.BlockSpec(memory_space=pltpu.SMEM)]
        + [VMEM_SPEC] * 3
        + [ANY_SPEC] * 4,
        out_specs=ANY_SPEC,
        scratch_shapes=[
            pltpu.VMEM((span, kv_width), BF16),
            pltpu.VMEM((span, kv_width), BF16),
            pltpu.VMEM((rows, span), jnp.int32),
            pltpu.VMEM((width // HEAD, rows, HEAD), F32),
            pltpu.VMEM((own, width), F32),
            pltpu.VMEM((all_rows, width), BF16),
            pltpu.VMEM((n_tp, own, HEAD), F32),
            pltpu.VMEM((own, HEAD), F32),
            pltpu.VMEM((n_ctx, depth, w_cols), BF16),
            pltpu.VMEM((n_ctx,) + w_out.shape, BF16),
            pltpu.VMEM((all_rows, w_cols), F32),
            pltpu.VMEM((n_ctx, all_rows, 2 * HEAD), BF16),
            pltpu.VMEM((heads, all_rows, HEAD), BF16),
            pltpu.VMEM((heads, all_rows, 1), F32),
            pltpu.VMEM((heads, all_rows, 1), F32),
            pltpu.VMEM((heads, all_rows, HEAD), F32),
            pltpu.VMEM((all_rows, q_width), BF16),
            pltpu.VMEM((all_rows // 2, width), BF16),
            pltpu.VMEM((all_rows // 2, width), BF16),
            pltpu.VMEM((all_rows // 2, width), BF16),
            pltpu.VMEM((all_rows // 2, width), BF16),
            pltpu.VMEM((all_rows // 2, width), BF16),
            pltpu.VMEM((own, width), F32),
            pltpu.VMEM((8, width // 8), F32),
            pltpu.VMEM((8, width // 8), F32),
            dma((2, CHUNKS, reach)),
            dma((2, CHUNKS, reach)),
            dma((CHUNKS, RING)),
            dma((CHUNKS, n_tp)),
            dma((CHUNKS, RING)),
            dma((2, RING)),
            dma((n_tp,)),
            dma((3, 4)),
            dma((2, 2, n_ctx, 4)),
            dma((2, 2, n_ctx)),
            dma((n_ctx,)),
            dma((n_ctx,)),
            dma((GROUPS,)),
            dma((GROUPS,)),
            dma((GROUPS, RING)),
            dma((GROUPS, RING)),
            dma((2,)),
            dma((width // HEAD,)),
        ],
        compiler_params=pltpu.CompilerParams(
            collective_id=0, has_side_effects=True, vmem_limit_bytes=62 * 2**20
        ),
        name="hourglass",
    )(
        fine_q, fine_k, fine_v, fine_x, windows, pool_w, norm_gain[None], up_w,
        w_query, w_key, w_value, w_out,
    )


def solution(mesh):
    placed = (
        P(("ctx", "tp"), None),
        P(("ctx", "tp"), None),
        P(("ctx", "tp"), None),
        P(("ctx", "tp"), None),
        P(),
        P(),
        P(),
        P("ctx", "tp"),
        P("ctx", "tp"),
        P("ctx", "tp"),
        P("tp", "ctx"),
        P(),
    )
    return jax.shard_map(
        functools.partial(per_device, mesh),
        mesh=mesh,
        in_specs=placed,
        out_specs=P(("ctx", "tp"), None),
        check_vma=False,
    )
```

```python
import functools

import jax
import jax.numpy as jnp
from jax import lax
from jax.experimental import pallas as pl
from jax.experimental.pallas import tpu as pltpu
from jax.sharding import PartitionSpec as P

HEAD = 128
WIN = 512
POOL = 4
RING = 4
LOG2E = 1.4426950408889634
MESH = pl.DeviceIdType.MESH
F32 = jnp.float32
BF16 = jnp.bfloat16
VMEM_SPEC = pl.BlockSpec(memory_space=pltpu.VMEM)
ANY_SPEC = pl.BlockSpec(memory_space=pl.ANY)
CHUNKS = 4
SLOTS = 4


def lanes(start, size):
    return pl.ds(pl.multiple_of(start, 128), size)


def sublanes(start, size):
    return pl.ds(pl.multiple_of(start, size), size)


def block_kernel(
    q_ref, k_ref, v_ref, x_ref, win_ref, pw_ref, gain_ref, up_ref, wq_hbm, wk_hbm, wv_hbm, wo_hbm,
    out_hbm,
    kbuf, vbuf, dist, stream, pooled_v, a_own, a_full, rs_all, ssq,
    w_all, wo_all, kv_part, q_part, kv_got, q_got, kv_all, q_all, top, total, mixed, h_all,
    keep, s_send, s_got, y_send, y_got, ring_sum, z_send, z_got, shifted, last_send, last_got,
    hs_sem, hr_sem, azs_sem, azr_sem, ays_sem, ayr_sem, acs_sem, rss_sem, rsr_sem,
    ho_sem, wgs_sem, wgr_sem, ps_sem, pr_sem, kvs_sem, kvr_sem, hzs_sem, hzr_sem,
    ss_sem, sr_sem, ys_sem, yr_sem, zs_sem, zr_sem, l_sem, o_sem,
):
    rows, width = q_ref.shape
    kv_width = k_ref.shape[1]
    reach = WIN // rows
    span = (reach + 1) * rows
    group = width // kv_width
    own = rows // POOL
    kv_chunk = kv_width // CHUNKS
    q_chunk = width // CHUNKS
    depth = w_all.shape[0] // SLOTS
    q_width = h_all.shape[2]
    heads = q_width // HEAD
    all_rows = h_all.shape[1]
    n_tp = 2 * RING
    n_ctx = 4 * RING
    n_dev = n_ctx * n_tp

    ctx = lax.axis_index("ctx")
    tp = lax.axis_index("tp")
    me = ctx * n_tp + tp
    x_lo = ctx // n_tp
    z = lax.rem(ctx, n_tp) // 2
    core = lax.rem(ctx, 2)
    x_hi = tp // RING
    y = lax.rem(tp, RING)
    x = 2 * x_hi + x_lo
    pair = x_lo * RING + z
    mine = pair * 2 + x_hi
    slot = core * RING + y

    def at(x_at, z_at, y_at, core_at):
        return (lax.rem(x_at, 2) * n_tp + z_at * 2 + core_at, (x_at // 2) * RING + y_at)

    def along(step):
        other = lax.rem(me + step + n_dev, n_dev)
        return (other // n_tp, lax.rem(other, n_tp))

    def turn(value, step):
        return lax.rem(value + step + 2 * RING, RING)

    def y_dev(step):
        return at(x, z, turn(y, step), core)

    def z_dev(step):
        return at(x, turn(z, step), y, core)

    def group_dev(g):
        p = g // 2
        return at(2 * lax.rem(g, 2) + p // RING, lax.rem(p, RING), y, core)

    sibling = at(x, z, y, 1 - core)

    def remote(src, dst, send_sem, recv_sem, device):
        return pltpu.make_async_remote_copy(
            src_ref=src, dst_ref=dst, send_sem=send_sem, recv_sem=recv_sem,
            device_id=device, device_id_type=MESH,
        )

    barrier = pltpu.get_barrier_semaphore()

    def greet(device):
        pl.semaphore_signal(barrier, inc=1, device_id=device, device_id_type=MESH)

    for e in range(1, RING):
        greet(y_dev(e))
        greet(at(x, z, turn(y, e), 1 - core))
    greet(sibling)
    greet(along(-reach))
    greet(along(-1))

    def greet_plane(d, carry):
        greet(group_dev(lax.rem(mine + d, n_ctx)))
        return carry

    lax.fori_loop(1, n_ctx, greet_plane, 0)
    pl.semaphore_wait(barrier, 2 * RING + 1 + n_ctx - 1)

    def block_cols(hc):
        return lanes(hc * kv_chunk, kv_chunk)

    def halo_copy(which, hc, d, device, source):
        buf = (kbuf, vbuf)[which]
        return remote(
            buf.at[sublanes(source * rows, rows), block_cols(hc)],
            buf.at[pl.ds((reach - d) * rows, rows), block_cols(hc)],
            hs_sem.at[which, hc, d - 1],
            hr_sem.at[which, hc, d - 1],
            device,
        )

    def halo_far(which, hc):
        return halo_copy(which, hc, reach, along(reach), reach)

    def halo_near(which, hc, e):
        return halo_copy(which, hc, e, y_dev(e), jnp.where(y + e < RING, reach, 0))

    kbuf[reach * rows :, :] = k_ref[...]
    vbuf[reach * rows :, :] = v_ref[...]
    for hc in range(CHUNKS):
        for which in range(2):
            halo_far(which, hc).start()

    is_home = core == x_hi

    def shard_parts(core_at):
        to = x_lo * 2 + core_at
        rows_to = sublanes(to * depth, depth)
        return (
            (wq_hbm, w_all.at[rows_to, 0:q_width]),
            (wk_hbm, w_all.at[rows_to, q_width : q_width + HEAD]),
            (wv_hbm, w_all.at[rows_to, q_width + HEAD : q_width + 2 * HEAD]),
            (wo_hbm, wo_all.at[to]),
        )

    def hand_over(i):
        src, dst = shard_parts(core)[i]
        return remote(src, dst, ho_sem.at[0, i], ho_sem.at[1, i], sibling)

    def hand_over_arrival(i):
        src, dst = shard_parts(1 - core)[i]
        return remote(src, dst, ho_sem.at[0, i], ho_sem.at[1, i], sibling)

    def stay(i):
        src, dst = shard_parts(core)[i]
        return pltpu.make_async_copy(src, dst, ho_sem.at[2, i])

    @pl.when(is_home)
    def _():
        for i in range(4):
            stay(i).start()

    @pl.when(jnp.logical_not(is_home))
    def _():
        for i in range(4):
            hand_over(i).start()

    for hc in range(CHUNKS):
        for which in range(2):
            for e in range(1, RING):

                @pl.when(y + e < RING)
                def _():
                    halo_near(which, hc, e).start()

    def hop(kind, k, lane):
        piece = w_all.at[sublanes(k * depth, depth)] if kind == 0 else wo_all.at[k]
        device = at(turn(x, 1 if lane == 0 else -1), z, y, core)
        return remote(piece, piece, wgs_sem.at[kind, k, lane], wgr_sem.at[kind, k], device)

    def off_x(k):
        return turn(x, -2 * core - k // 2)

    def hop_wanted(k, lane):
        onward = (off_x(k) == 1) & (lax.rem(k, 2) == 0)
        back = (off_x(k) == 3) & (lax.rem(k, 2) == 1)
        return (off_x(k) == 0) | (onward if lane == 0 else back)

    def launch(kind, k):
        for lane in range(2):

            @pl.when(hop_wanted(k, lane))
            def _():
                hop(kind, k, lane).start()

    def origin(kind):
        @pl.when(is_home)
        def _():
            for i in range(4):
                if (i == 3) == (kind == 1):
                    stay(i).wait()
                    hand_over_arrival(i).wait_recv()
            for c in range(2):
                launch(kind, x_lo * 2 + c)

    def relay(kind):
        def one(k, carry):
            @pl.when((off_x(k) == 1) | (off_x(k) == 3))
            def _():
                hop(kind, k, 0).wait_recv()
                launch(kind, k)

            return carry

        lax.fori_loop(0, SLOTS, one, 0)

    def finish(kind):
        def one(k, carry):
            @pl.when(off_x(k) == 2)
            def _():
                hop(kind, k, 0).wait_recv()

            return carry

        lax.fori_loop(0, SLOTS, one, 0)

    def settle(kind):
        def one(k, carry):
            for lane in range(2):

                @pl.when(hop_wanted(k, lane))
                def _():
                    hop(kind, k, lane).wait_send()

            return carry

        lax.fori_loop(0, SLOTS, one, 0)

    origin(0)

    for hc in range(CHUNKS):
        for which in range(2):
            halo_far(which, hc).wait_recv()
        for which in range(2):
            for e in range(1, RING):

                @pl.when(y + e >= RING)
                def _():
                    halo_near(which, hc, e).start()

    q_at = lax.broadcasted_iota(jnp.int32, (rows, span), 0)
    l_at = lax.broadcasted_iota(jnp.int32, (rows, span), 1)
    gap = reach * rows + q_at - l_at
    outside = (gap < 0) | (l_at < (reach - me) * rows)
    dist[...] = jnp.where(outside, 2 * span, gap)
    ssq[...] = jnp.zeros_like(ssq)

    def a_rows(s):
        return sublanes(s * own, own)

    piece_cols = q_chunk // 2
    block_rows = RING * own

    def a_z_copy(hc, p):
        to = lax.rem(hc, 2) * 2 + p
        return remote(
            a_own.at[:, lanes(hc * q_chunk + p * piece_cols, piece_cols)],
            a_full.at[a_rows(slot * RING + z), lanes((hc // 2) * piece_cols, piece_cols)],
            azs_sem.at[hc, p],
            azr_sem.at[hc // 2, z],
            at(x, to, y, core),
        )

    def a_z_arrival(j, e):
        source = turn(z, e)
        piece = a_full.at[a_rows(slot * RING + source), lanes(j * piece_cols, piece_cols)]
        return remote(piece, piece, azs_sem.at[0, 0], azr_sem.at[j, source], z_dev(e))

    def a_block(j, s):
        return a_full.at[sublanes(s * block_rows, block_rows), lanes(j * piece_cols, piece_cols)]

    def a_copy(j, e):
        device = sibling if e == 0 else y_dev(e)
        return remote(
            a_block(j, slot), a_block(j, slot), ays_sem.at[j, e], ayr_sem.at[j, slot], device
        )

    def a_onward(j, e):
        s = core * RING + turn(y, -e)
        return remote(a_block(j, s), a_block(j, s), acs_sem.at[j, e], ayr_sem.at[j, s], sibling)

    def a_other(j, y_at):
        s = (1 - core) * RING + y_at
        return remote(a_block(j, s), a_block(j, s), acs_sem.at[j, 0], ayr_sem.at[j, s], sibling)

    def a_relay(j):
        for e in range(1, RING):
            a_z_arrival(j, e).wait_recv()
        for e in range(RING):
            a_copy(j, e).start()

    part_heads = group // 2

    def chunk(hc, carry):
        for which in range(2):
            for e in range(1, RING):
                halo_near(which, hc, e).wait_recv()
        for u in range(kv_chunk // HEAD):
            kv_cols = lanes(hc * kv_chunk + u * HEAD, HEAD)
            keys = kbuf[:, kv_cols]
            values = vbuf[:, kv_cols]
            for part in range(2):
                first = (hc * (kv_chunk // HEAD) + u) * group + part * part_heads
                qs = jnp.concatenate(
                    [q_ref[:, lanes((first + i) * HEAD, HEAD)] for i in range(part_heads)], axis=0
                )
                scores = lax.dot_general(
                    qs, keys, (((1,), (1,)), ((), ())), preferred_element_type=F32
                )
                weights, totals = [], []
                for i in range(part_heads):
                    s = scores[i * rows : (i + 1) * rows] * (LOG2E * HEAD**-0.5)
                    s = jnp.where(dist[...] < win_ref[first + i], s, -1e30)
                    p = jnp.exp2(s - s.max(-1, keepdims=True))
                    totals.append(p.sum(-1, keepdims=True))
                    weights.append(p.astype(BF16))
                out = jnp.dot(
                    jnp.concatenate(weights, axis=0), values, preferred_element_type=F32
                )
                for i in range(part_heads):
                    cols = lanes((first + i) * HEAD, HEAD)
                    stream[first + i] = (
                        x_ref[:, cols].astype(F32) + out[i * rows : (i + 1) * rows] / totals[i]
                    )
        for i in range(q_chunk // HEAD):
            cols = lanes(hc * q_chunk + i * HEAD, HEAD)
            head = hc * (q_chunk // HEAD) + i
            pooled = sum(
                pw_ref[j : j + 1, cols] * stream[head, pl.ds(j, own, stride=POOL), :]
                for j in range(POOL)
            )
            pooled_v[:, cols] = pooled
            ssq[...] += pooled * pooled
            a_own[:, cols] = (pooled * gain_ref[:, cols]).astype(BF16)
        for p in range(2):
            to = lax.rem(hc, 2) * 2 + p

            @pl.when(to != z)
            def _():
                a_z_copy(hc, p).start()

            @pl.when(to == z)
            def _():
                a_full[a_rows(slot * RING + z), lanes((hc // 2) * piece_cols, piece_cols)] = a_own[
                    :, lanes(hc * q_chunk + p * piece_cols, piece_cols)
                ]

        @pl.when(hc == 1)
        def _():
            relay(0)
            origin(1)

        @pl.when(hc == 2)
        def _():
            a_relay(0)

        @pl.when(hc == 3)
        def _():
            relay(1)

        return carry

    lax.fori_loop(0, CHUNKS, chunk, 0)

    mean = ssq[...].sum(-1, keepdims=True) * (1.0 / width)
    rs_all[slot] = jnp.broadcast_to(lax.rsqrt(mean + 1e-05), ssq.shape)

    def rs_copy(e, other):
        device = at(x, z, turn(y, e), 1 - core if other else core)
        return remote(
            rs_all.at[slot], rs_all.at[slot], rss_sem.at[other, e], rsr_sem.at[slot], device
        )

    def rs_arrival(e, other):
        s = (1 - core if other else core) * RING + turn(y, e)
        return remote(
            rs_all.at[s], rs_all.at[s], rss_sem.at[other, e], rsr_sem.at[s], sibling
        )

    others = [(e, other) for other in range(2) for e in range(RING) if (e, other) != (0, 0)]
    for e, other in others:
        rs_copy(e, other).start()

    a_relay(1)
    for j in range(2):
        for e in range(1, RING):
            a_onward(j, e).wait_recv()
            a_onward(j, e).start()
    finish(0)
    for j in range(2):
        for y_at in range(RING):
            a_other(j, y_at).wait_recv()
    for e, other in others:
        rs_arrival(e, other).wait_recv()

    def part_copy(kind, e):
        part, got = ((kv_part, kv_got), (q_part, q_got))[kind]
        return remote(
            part.at[turn(z, e)], got.at[z], ps_sem.at[kind, e], pr_sem.at[kind, z], z_dev(e)
        )

    def part_arrival(kind, e):
        part, got = ((kv_part, kv_got), (q_part, q_got))[kind]
        source = turn(z, e)
        return remote(
            part.at[source], got.at[source], ps_sem.at[kind, e], pr_sem.at[kind, source], z_dev(e)
        )

    def project(kind):
        part = (kv_part, q_part)[kind]
        cols = (slice(q_width, None), slice(0, q_width))[kind]

        def one(m, carry):
            product = jnp.dot(
                a_full[sublanes(m * all_rows, all_rows), :], w_all[:, cols], preferred_element_type=F32
            ).astype(BF16)
            for i in range(2):
                for zz in range(RING):
                    first = (i * RING + zz) * own
                    part[zz, a_rows(m * 2 + i), :] = product[first : first + own]
            return carry

        lax.fori_loop(0, RING, one, 0)
        for e in range(1, RING):
            part_copy(kind, e).start()

    def part_sum(kind):
        part, got = ((kv_part, kv_got), (q_part, q_got))[kind]
        value = part[z].astype(F32)
        for e in range(1, RING):
            part_arrival(kind, e).wait_recv()
            value += got[turn(z, e)].astype(F32)
        return value

    project(0)
    project(1)
    row_scale = jnp.concatenate([rs_all[s] for s in range(n_tp)], axis=0)[:, 0:1]
    kv_all[mine] = (part_sum(0) * row_scale).astype(BF16)

    def kv_copy(to):
        return remote(
            kv_all.at[mine], kv_all.at[mine], kvs_sem.at[to], kvr_sem.at[mine], group_dev(to)
        )

    def kv_arrival(source):
        return remote(
            kv_all.at[source], kv_all.at[source], kvs_sem.at[source], kvr_sem.at[source],
            group_dev(source),
        )

    partner = pair * 2 + 1 - x_hi

    def kv_send(to, carry):
        kv_copy(to).start()
        return carry

    kv_copy(partner).start()
    lax.fori_loop(pair * 2 + 2, n_ctx, kv_send, 0)
    q_rows = (part_sum(1) * row_scale).astype(BF16)
    for h in range(heads):
        q_all[h] = q_rows[:, h * HEAD : (h + 1) * HEAD]

    def attend(b, first):
        keys = jnp.concatenate([kv_all[2 * b, :, :HEAD], kv_all[2 * b + 1, :, :HEAD]], axis=0)
        values = jnp.concatenate([kv_all[2 * b, :, HEAD:], kv_all[2 * b + 1, :, HEAD:]], axis=0)
        for h in range(heads):
            s = lax.dot_general(
                q_all[h], keys, (((1,), (1,)), ((), ())), preferred_element_type=F32
            ) * (LOG2E * HEAD**-0.5)
            if first:
                run = all_rows // 2
                row = lax.broadcasted_iota(jnp.int32, s.shape, 0)
                col = lax.broadcasted_iota(jnp.int32, s.shape, 1)
                q_pos = row + x_hi * run + jnp.where(row >= run, run, 0)
                in_block = jnp.where(col >= all_rows, col - all_rows, col)
                k_pos = (
                    in_block + jnp.where(col >= all_rows, run, 0) + jnp.where(in_block >= run, run, 0)
                )
                s = jnp.where(k_pos <= q_pos, s, -1e30)
                new_top = s.max(-1, keepdims=True)
                p = jnp.exp2(s - new_top)
                total[h] = p.sum(-1, keepdims=True)
                mixed[h] = jnp.dot(p.astype(BF16), values, preferred_element_type=F32)
            else:
                old = top[h]
                new_top = jnp.maximum(old, s.max(-1, keepdims=True))
                scale = jnp.exp2(old - new_top)
                p = jnp.exp2(s - new_top)
                total[h] = total[h] * scale + p.sum(-1, keepdims=True)
                mixed[h] = mixed[h] * scale + jnp.dot(
                    p.astype(BF16), values, preferred_element_type=F32
                )
            top[h] = new_top

    kv_arrival(partner).wait_recv()
    attend(pair, True)

    def earlier(b, carry):
        kv_arrival(2 * b).wait_recv()
        kv_arrival(2 * b + 1).wait_recv()
        attend(b, False)
        return carry

    lax.fori_loop(0, pair, earlier, 0)
    for h in range(heads):
        h_all[z, :, h * HEAD : (h + 1) * HEAD] = (mixed[h] / total[h]).astype(BF16)

    def h_copy(e):
        return remote(h_all.at[z], h_all.at[z], hzs_sem.at[e], hzr_sem.at[z], z_dev(e))

    def h_arrival(e):
        source = turn(z, e)
        return remote(h_all.at[source], h_all.at[source], hzs_sem.at[e], hzr_sem.at[source], z_dev(e))

    for e in range(1, RING):
        h_copy(e).start()
    finish(1)
    for e in range(1, RING):
        h_arrival(e).wait_recv()

    cols_out = wo_all.shape[2]

    def out_cols(g):
        return lanes(g * cols_out, cols_out)

    def s_copy(g):
        return remote(
            s_send.at[:, out_cols(g)], s_got.at[:, out_cols(g)], ss_sem.at[g], sr_sem.at[g], sibling
        )

    def multiply(g, carry):
        for zz in range(RING):
            product = jnp.dot(h_all[zz], wo_all[g], preferred_element_type=F32)
            low, high = product[: all_rows // 2], product[all_rows // 2 :]
            stays = jnp.where(core == 0, low, high).astype(BF16)
            goes = jnp.where(core == 0, high, low).astype(BF16)
            for yy in range(RING):
                at_rows = a_rows(yy * RING + zz)
                keep[at_rows, out_cols(g)] = stays[yy * own : (yy + 1) * own]
                s_send[at_rows, out_cols(g)] = goes[yy * own : (yy + 1) * own]
        s_copy(g).start()
        return carry

    lax.fori_loop(0, SLOTS, multiply, 0)

    def y_rows(y_at):
        return sublanes(y_at * block_rows, block_rows)

    def y_copy(g, e):
        return remote(
            y_send.at[y_rows(turn(y, e)), out_cols(g)], y_got.at[y_rows(y), out_cols(g)],
            ys_sem.at[g, e], yr_sem.at[g, y], y_dev(e),
        )

    def y_arrival(g, e):
        source = turn(y, e)
        return remote(
            y_send.at[y_rows(source), out_cols(g)], y_got.at[y_rows(source), out_cols(g)],
            ys_sem.at[g, e], yr_sem.at[g, source], y_dev(e),
        )

    def reduce_cores(g, carry):
        where = out_cols(g)
        s_copy(g).wait_recv()
        y_send[:, where] = (keep[:, where].astype(F32) + s_got[:, where].astype(F32)).astype(BF16)
        for e in range(1, RING):
            y_copy(g, e).start()
        ring_sum[:, where] = (
            keep[y_rows(y), where].astype(F32) + s_got[y_rows(y), where].astype(F32)
        )
        return carry

    lax.fori_loop(0, SLOTS, reduce_cores, 0)

    def z_copy(g, e):
        return remote(
            z_send.at[a_rows(turn(z, e)), out_cols(g)], z_got.at[a_rows(z), out_cols(g)],
            zs_sem.at[g, e], zr_sem.at[g, z], z_dev(e),
        )

    def z_arrival(g, e):
        source = turn(z, e)
        return remote(
            z_send.at[a_rows(source), out_cols(g)], z_got.at[a_rows(source), out_cols(g)],
            zs_sem.at[g, e], zr_sem.at[g, source], z_dev(e),
        )

    def full_cols(g, z_at):
        return lanes(((g // 2) * n_tp + z_at * 2 + lax.rem(g, 2)) * cols_out, cols_out)

    def reduce_ring(g, carry):
        where = out_cols(g)
        for e in range(1, RING):
            y_arrival(g, e).wait_recv()
        value = ring_sum[:, where]
        for e in range(1, RING):
            value += y_got[y_rows(turn(y, e)), where].astype(F32)
        ring_sum[:, where] = value
        z_send[:, where] = value.astype(BF16)
        for e in range(1, RING):
            z_copy(g, e).start()
        pooled_v[:, full_cols(g, z)] += ring_sum[a_rows(z), where]
        return carry

    lax.fori_loop(0, SLOTS, reduce_ring, 0)

    def take_home(g, carry):
        for e in range(1, RING):
            z_arrival(g, e).wait_recv()
            source = turn(z, e)
            pooled_v[:, full_cols(g, source)] += z_got[a_rows(source), out_cols(g)].astype(F32)
        return carry

    lax.fori_loop(0, SLOTS, take_home, 0)

    piece = last_send.shape[1]
    for i in range(last_send.shape[0]):
        last_send[i : i + 1, :] = pooled_v[own - 1 : own, i * piece : (i + 1) * piece]
    last = remote(last_send, last_got, l_sem.at[0], l_sem.at[1], along(1))
    last.start()
    shifted[1:own, :] = pooled_v[0 : own - 1, :]
    last.wait()
    first_row = jnp.where(me == 0, 0.0, last_got[...])
    for i in range(last_send.shape[0]):
        shifted[0:1, i * piece : (i + 1) * piece] = first_row[i : i + 1, :]

    def result(h):
        return pltpu.make_async_copy(
            stream.at[h], out_hbm.at[:, lanes(h * HEAD, HEAD)], o_sem.at[h]
        )

    def combine(i, carry):
        for u in range(group):
            h = i * group + u
            cols = lanes(h * HEAD, HEAD)
            add = shifted[:, cols]
            for j in range(POOL):
                where = pl.ds(j, own, stride=POOL)
                stream[h, where, :] = stream[h, where, :] + up_ref[j : j + 1, cols] * add
            result(h).start()
        return carry

    lax.fori_loop(0, width // HEAD // group, combine, 0)

    for hc in range(CHUNKS):
        for which in range(2):
            halo_far(which, hc).wait_send()
            for e in range(1, RING):
                halo_near(which, hc, e).wait_send()

    @pl.when(jnp.logical_not(is_home))
    def _():
        for i in range(4):
            hand_over(i).wait_send()

    settle(0)
    settle(1)

    def a_settle(hc, carry):
        for p in range(2):

            @pl.when(lax.rem(hc, 2) * 2 + p != z)
            def _():
                a_z_copy(hc, p).wait_send()

        return carry

    lax.fori_loop(0, CHUNKS, a_settle, 0)
    for j in range(2):
        for e in range(RING):
            a_copy(j, e).wait_send()
        for e in range(1, RING):
            a_onward(j, e).wait_send()
    for e in range(1, RING):
        part_copy(0, e).wait_send()
        part_copy(1, e).wait_send()
        h_copy(e).wait_send()
    for e, other in others:
        rs_copy(e, other).wait_send()

    def kv_settle(to, carry):
        kv_copy(to).wait_send()
        return carry

    kv_copy(partner).wait_send()
    lax.fori_loop(pair * 2 + 2, n_ctx, kv_settle, 0)

    def sums_settle(g, carry):
        s_copy(g).wait_send()
        for e in range(1, RING):
            y_copy(g, e).wait_send()
            z_copy(g, e).wait_send()
        return carry

    lax.fori_loop(0, SLOTS, sums_settle, 0)

    def out_settle(h, carry):
        result(h).wait()
        return carry

    lax.fori_loop(0, width // HEAD, out_settle, 0)


def per_device(
    mesh, fine_x, fine_q, fine_k, fine_v, windows, pool_w, norm_gain, w_query, w_key, w_value, w_out, up_w
):
    rows, width = fine_q.shape
    kv_width = fine_k.shape[1]
    n_tp, n_ctx = mesh.shape["tp"], mesh.shape["ctx"]
    reach = WIN // rows
    span = (reach + 1) * rows
    own = rows // POOL
    all_rows = own * n_tp
    depth, q_width = w_query.shape
    heads = q_width // HEAD
    w_cols = q_width + 2 * HEAD
    dma = pltpu.SemaphoreType.DMA
    return pl.pallas_call(
        block_kernel,
        out_shape=jax.ShapeDtypeStruct((rows, width), F32),
        in_specs=[VMEM_SPEC] * 4
        + [pl.BlockSpec(memory_space=pltpu.SMEM)]
        + [VMEM_SPEC] * 3
        + [ANY_SPEC] * 4,
        out_specs=ANY_SPEC,
        scratch_shapes=[
            pltpu.VMEM((span, kv_width), BF16),
            pltpu.VMEM((span, kv_width), BF16),
            pltpu.VMEM((rows, span), jnp.int32),
            pltpu.VMEM((width // HEAD, rows, HEAD), F32),
            pltpu.VMEM((own, width), F32),
            pltpu.VMEM((own, width), BF16),
            pltpu.VMEM((RING * all_rows, width // RING), BF16),
            pltpu.VMEM((n_tp, own, HEAD), F32),
            pltpu.VMEM((own, HEAD), F32),
            pltpu.VMEM((SLOTS * depth, w_cols), BF16),
            pltpu.VMEM((SLOTS,) + w_out.shape, BF16),
            pltpu.VMEM((RING, all_rows, 2 * HEAD), BF16),
            pltpu.VMEM((RING, all_rows, q_width), BF16),
            pltpu.VMEM((RING, all_rows, 2 * HEAD), BF16),
            pltpu.VMEM((RING, all_rows, q_width), BF16),
            pltpu.VMEM((n_ctx, all_rows, 2 * HEAD), BF16),
            pltpu.VMEM((heads, all_rows, HEAD), BF16),
            pltpu.VMEM((heads, all_rows, 1), F32),
            pltpu.VMEM((heads, all_rows, 1), F32),
            pltpu.VMEM((heads, all_rows, HEAD), F32),
            pltpu.VMEM((RING, all_rows, q_width), BF16),
        ]
        + [pltpu.VMEM((RING * all_rows // 2, width // RING), BF16)] * 5
        + [
            pltpu.VMEM((RING * own, width // RING), F32),
            pltpu.VMEM((RING * own, width // RING), BF16),
            pltpu.VMEM((RING * own, width // RING), BF16),
            pltpu.VMEM((own, width), F32),
            pltpu.VMEM((8, width // 8), F32),
            pltpu.VMEM((8, width // 8), F32),
            dma((2, CHUNKS, reach)),
            dma((2, CHUNKS, reach)),
            dma((CHUNKS, 2)),
            dma((2, RING)),
            dma((2, RING)),
            dma((2, n_tp)),
            dma((2, RING)),
            dma((2, RING)),
            dma((n_tp,)),
            dma((3, 4)),
            dma((2, SLOTS, 2)),
            dma((2, SLOTS)),
            dma((2, RING)),
            dma((2, RING)),
            dma((n_ctx,)),
            dma((n_ctx,)),
            dma((RING,)),
            dma((RING,)),
            dma((SLOTS,)),
            dma((SLOTS,)),
            dma((SLOTS, RING)),
            dma((SLOTS, RING)),
            dma((SLOTS, RING)),
            dma((SLOTS, RING)),
            dma((2,)),
            dma((width // HEAD,)),
        ],
        compiler_params=pltpu.CompilerParams(
            collective_id=0, has_side_effects=True, vmem_limit_bytes=62 * 2**20
        ),
        name="hourglass",
    )(
        fine_q, fine_k, fine_v, fine_x, windows, pool_w, norm_gain[None], up_w,
        w_query, w_key, w_value, w_out,
    )


def solution(mesh):
    placed = (
        P(("ctx", "tp"), None),
        P(("ctx", "tp"), None),
        P(("ctx", "tp"), None),
        P(("ctx", "tp"), None),
        P(),
        P(),
        P(),
        P("ctx", "tp"),
        P("ctx", "tp"),
        P("ctx", "tp"),
        P("tp", "ctx"),
        P(),
    )
    return jax.shard_map(
        functools.partial(per_device, mesh),
        mesh=mesh,
        in_specs=placed,
        out_specs=P(("ctx", "tp"), None),
        check_vma=False,
    )
```

```python
import functools

import jax
import jax.numpy as jnp
from jax import lax
from jax.experimental import pallas as pl
from jax.experimental.pallas import tpu as pltpu
from jax.sharding import PartitionSpec as P

HEAD = 128
WIN = 512
POOL = 4
RING = 4
LOG2E = 1.4426950408889634
MESH = pl.DeviceIdType.MESH
F32 = jnp.float32
BF16 = jnp.bfloat16
VMEM_SPEC = pl.BlockSpec(memory_space=pltpu.VMEM)
ANY_SPEC = pl.BlockSpec(memory_space=pl.ANY)
CHUNKS = 4
SLOTS = 4


def lanes(start, size):
    return pl.ds(pl.multiple_of(start, 128), size)


def sublanes(start, size):
    return pl.ds(pl.multiple_of(start, size), size)


def block_kernel(
    q_hbm, k_hbm, v_hbm, x_hbm, win_ref, pw_ref, gain_ref, up_ref, wq_hbm, wk_hbm, wv_hbm, wo_hbm,
    out_hbm,
    q_ref, x_ref, kbuf, vbuf, dist, stream, pooled_v, a_own, a_full, rs_all, ssq,
    w_all, wo_all, kv_part, q_part, kv_got, q_got, kv_all, q_all, top, total, mixed, h_all,
    keep, s_send, s_got, y_send, y_got, ring_sum, z_send, z_got, shifted, last_send, last_got,
    in_sem, hs_sem, hr_sem, azs_sem, azr_sem, ays_sem, ayr_sem, acs_sem, rss_sem, rsr_sem,
    ho_sem, wgs_sem, wgr_sem, ps_sem, pr_sem, kvs_sem, kvr_sem, hzs_sem, hzr_sem,
    ss_sem, sr_sem, ys_sem, yr_sem, zs_sem, zr_sem, l_sem, o_sem,
):
    rows, width = q_ref.shape
    kv_width = kbuf.shape[1]
    reach = WIN // rows
    span = (reach + 1) * rows
    group = width // kv_width
    own = rows // POOL
    kv_chunk = kv_width // CHUNKS
    q_chunk = width // CHUNKS
    depth = w_all.shape[0] // SLOTS
    q_width = h_all.shape[2]
    heads = q_width // HEAD
    all_rows = h_all.shape[1]
    n_tp = 2 * RING
    n_ctx = 4 * RING
    n_dev = n_ctx * n_tp

    ctx = lax.axis_index("ctx")
    tp = lax.axis_index("tp")
    me = ctx * n_tp + tp
    x_lo = ctx // n_tp
    z = lax.rem(ctx, n_tp) // 2
    core = lax.rem(ctx, 2)
    x_hi = tp // RING
    y = lax.rem(tp, RING)
    x = 2 * x_hi + x_lo
    pair = x_lo * RING + z
    mine = pair * 2 + x_hi
    slot = core * RING + y

    def at(x_at, z_at, y_at, core_at):
        return (lax.rem(x_at, 2) * n_tp + z_at * 2 + core_at, (x_at // 2) * RING + y_at)

    def along(step):
        other = lax.rem(me + step + n_dev, n_dev)
        return (other // n_tp, lax.rem(other, n_tp))

    def turn(value, step):
        return lax.rem(value + step + 2 * RING, RING)

    def y_dev(step):
        return at(x, z, turn(y, step), core)

    def z_dev(step):
        return at(x, turn(z, step), y, core)

    def group_dev(g):
        p = g // 2
        return at(2 * lax.rem(g, 2) + p // RING, lax.rem(p, RING), y, core)

    sibling = at(x, z, y, 1 - core)

    def remote(src, dst, send_sem, recv_sem, device):
        return pltpu.make_async_remote_copy(
            src_ref=src, dst_ref=dst, send_sem=send_sem, recv_sem=recv_sem,
            device_id=device, device_id_type=MESH,
        )

    last_rows = pl.ds(reach * rows, rows)
    loads = [
        pltpu.make_async_copy(src, dst, in_sem.at[i])
        for i, (src, dst) in enumerate(
            ((k_hbm, kbuf.at[last_rows]), (v_hbm, vbuf.at[last_rows]), (q_hbm, q_ref), (x_hbm, x_ref))
        )
    ]
    for load in loads:
        load.start()
    barrier = pltpu.get_barrier_semaphore()

    def greet(device):
        pl.semaphore_signal(barrier, inc=1, device_id=device, device_id_type=MESH)

    for e in range(1, RING):
        greet(y_dev(e))
        greet(at(x, z, turn(y, e), 1 - core))
    greet(sibling)
    greet(along(-reach))
    greet(along(-1))

    def greet_plane(d, carry):
        greet(group_dev(lax.rem(mine + d, n_ctx)))
        return carry

    lax.fori_loop(1, n_ctx, greet_plane, 0)
    pl.semaphore_wait(barrier, 2 * RING + 1 + n_ctx - 1)

    def block_cols(hc):
        return lanes(hc * kv_chunk, kv_chunk)

    def halo_copy(which, hc, d, device, source):
        buf = (kbuf, vbuf)[which]
        return remote(
            buf.at[sublanes(source * rows, rows), block_cols(hc)],
            buf.at[pl.ds((reach - d) * rows, rows), block_cols(hc)],
            hs_sem.at[which, hc, d - 1],
            hr_sem.at[which, hc, d - 1],
            device,
        )

    def halo_far(which, hc):
        return halo_copy(which, hc, reach, along(reach), reach)

    def halo_near(which, hc, e):
        return halo_copy(which, hc, e, y_dev(e), jnp.where(y + e < RING, reach, 0))

    loads[0].wait()
    loads[1].wait()
    for hc in range(CHUNKS):
        for which in range(2):
            halo_far(which, hc).start()

    is_home = core == x_hi

    def shard_parts(core_at):
        to = x_lo * 2 + core_at
        rows_to = sublanes(to * depth, depth)
        return (
            (wq_hbm, w_all.at[rows_to, 0:q_width]),
            (wk_hbm, w_all.at[rows_to, q_width : q_width + HEAD]),
            (wv_hbm, w_all.at[rows_to, q_width + HEAD : q_width + 2 * HEAD]),
            (wo_hbm, wo_all.at[to]),
        )

    def hand_over(i):
        src, dst = shard_parts(core)[i]
        return remote(src, dst, ho_sem.at[0, i], ho_sem.at[1, i], sibling)

    def hand_over_arrival(i):
        src, dst = shard_parts(1 - core)[i]
        return remote(src, dst, ho_sem.at[0, i], ho_sem.at[1, i], sibling)

    def stay(i):
        src, dst = shard_parts(core)[i]
        return pltpu.make_async_copy(src, dst, ho_sem.at[2, i])

    @pl.when(is_home)
    def _():
        for i in range(4):
            stay(i).start()

    @pl.when(jnp.logical_not(is_home))
    def _():
        for i in range(4):
            hand_over(i).start()

    for hc in range(CHUNKS):
        for which in range(2):
            for e in range(1, RING):

                @pl.when(y + e < RING)
                def _():
                    halo_near(which, hc, e).start()

    def hop(kind, k, lane):
        piece = w_all.at[sublanes(k * depth, depth)] if kind == 0 else wo_all.at[k]
        device = at(turn(x, 1 if lane == 0 else -1), z, y, core)
        return remote(piece, piece, wgs_sem.at[kind, k, lane], wgr_sem.at[kind, k], device)

    def off_x(k):
        return turn(x, -2 * core - k // 2)

    def hop_wanted(k, lane):
        onward = (off_x(k) == 1) & (lax.rem(k, 2) == 0)
        back = (off_x(k) == 3) & (lax.rem(k, 2) == 1)
        return (off_x(k) == 0) | (onward if lane == 0 else back)

    def launch(kind, k):
        for lane in range(2):

            @pl.when(hop_wanted(k, lane))
            def _():
                hop(kind, k, lane).start()

    def origin(kind):
        @pl.when(is_home)
        def _():
            for i in range(4):
                if (i == 3) == (kind == 1):
                    stay(i).wait()
                    hand_over_arrival(i).wait_recv()
            for c in range(2):
                launch(kind, x_lo * 2 + c)

    def relay(kind):
        def one(k, carry):
            @pl.when((off_x(k) == 1) | (off_x(k) == 3))
            def _():
                hop(kind, k, 0).wait_recv()
                launch(kind, k)

            return carry

        lax.fori_loop(0, SLOTS, one, 0)

    def finish(kind):
        def one(k, carry):
            @pl.when(off_x(k) == 2)
            def _():
                hop(kind, k, 0).wait_recv()

            return carry

        lax.fori_loop(0, SLOTS, one, 0)

    def settle(kind):
        def one(k, carry):
            for lane in range(2):

                @pl.when(hop_wanted(k, lane))
                def _():
                    hop(kind, k, lane).wait_send()

            return carry

        lax.fori_loop(0, SLOTS, one, 0)

    for hc in range(CHUNKS):
        for which in range(2):
            halo_far(which, hc).wait_recv()
        for which in range(2):
            for e in range(1, RING):

                @pl.when(y + e >= RING)
                def _():
                    halo_near(which, hc, e).start()

    origin(0)
    q_at = lax.broadcasted_iota(jnp.int32, (rows, span), 0)
    l_at = lax.broadcasted_iota(jnp.int32, (rows, span), 1)
    gap = reach * rows + q_at - l_at
    outside = (gap < 0) | (l_at < (reach - me) * rows)
    dist[...] = jnp.where(outside, 2 * span, gap)
    ssq[...] = jnp.zeros_like(ssq)

    def a_rows(s):
        return sublanes(s * own, own)

    piece_cols = q_chunk // 2
    block_rows = RING * own

    def a_z_copy(hc, p):
        to = lax.rem(hc, 2) * 2 + p
        return remote(
            a_own.at[:, lanes(hc * q_chunk + p * piece_cols, piece_cols)],
            a_full.at[a_rows(slot * RING + z), lanes((hc // 2) * piece_cols, piece_cols)],
            azs_sem.at[hc, p],
            azr_sem.at[hc // 2, z],
            at(x, to, y, core),
        )

    def a_z_arrival(j, e):
        source = turn(z, e)
        piece = a_full.at[a_rows(slot * RING + source), lanes(j * piece_cols, piece_cols)]
        return remote(piece, piece, azs_sem.at[0, 0], azr_sem.at[j, source], z_dev(e))

    def a_block(j, s):
        return a_full.at[sublanes(s * block_rows, block_rows), lanes(j * piece_cols, piece_cols)]

    def a_copy(j, e):
        device = sibling if e == 0 else y_dev(e)
        return remote(
            a_block(j, slot), a_block(j, slot), ays_sem.at[j, e], ayr_sem.at[j, slot], device
        )

    def a_onward(j, e):
        s = core * RING + turn(y, -e)
        return remote(a_block(j, s), a_block(j, s), acs_sem.at[j, e], ayr_sem.at[j, s], sibling)

    def a_other(j, y_at):
        s = (1 - core) * RING + y_at
        return remote(a_block(j, s), a_block(j, s), acs_sem.at[j, 0], ayr_sem.at[j, s], sibling)

    def a_relay(j):
        for e in range(1, RING):
            a_z_arrival(j, e).wait_recv()
        for e in range(RING):
            a_copy(j, e).start()

    part_heads = group // 2

    def chunk(hc, carry):
        for which in range(2):
            for e in range(1, RING):
                halo_near(which, hc, e).wait_recv()
        for u in range(kv_chunk // HEAD):
            kv_cols = lanes(hc * kv_chunk + u * HEAD, HEAD)
            keys = kbuf[:, kv_cols]
            values = vbuf[:, kv_cols]
            for part in range(2):
                first = (hc * (kv_chunk // HEAD) + u) * group + part * part_heads
                qs = jnp.concatenate(
                    [q_ref[:, lanes((first + i) * HEAD, HEAD)] for i in range(part_heads)], axis=0
                )
                scores = lax.dot_general(
                    qs, keys, (((1,), (1,)), ((), ())), preferred_element_type=F32
                )
                weights, totals = [], []
                for i in range(part_heads):
                    s = scores[i * rows : (i + 1) * rows] * (LOG2E * HEAD**-0.5)
                    s = jnp.where(dist[...] < win_ref[first + i], s, -1e30)
                    p = jnp.exp2(s - s.max(-1, keepdims=True))
                    totals.append(p.sum(-1, keepdims=True))
                    weights.append(p.astype(BF16))
                out = jnp.dot(
                    jnp.concatenate(weights, axis=0), values, preferred_element_type=F32
                )
                for i in range(part_heads):
                    cols = lanes((first + i) * HEAD, HEAD)
                    stream[first + i] = (
                        x_ref[:, cols].astype(F32) + out[i * rows : (i + 1) * rows] / totals[i]
                    )
        for i in range(q_chunk // HEAD):
            cols = lanes(hc * q_chunk + i * HEAD, HEAD)
            head = hc * (q_chunk // HEAD) + i
            pooled = sum(
                pw_ref[j : j + 1, cols] * stream[head, pl.ds(j, own, stride=POOL), :]
                for j in range(POOL)
            )
            pooled_v[:, cols] = pooled
            ssq[...] += pooled * pooled
            a_own[:, cols] = (pooled * gain_ref[:, cols]).astype(BF16)
        for p in range(2):
            to = lax.rem(hc, 2) * 2 + p

            @pl.when(to != z)
            def _():
                a_z_copy(hc, p).start()

            @pl.when(to == z)
            def _():
                a_full[a_rows(slot * RING + z), lanes((hc // 2) * piece_cols, piece_cols)] = a_own[
                    :, lanes(hc * q_chunk + p * piece_cols, piece_cols)
                ]

        @pl.when(hc == 2)
        def _():
            a_relay(0)

        return carry

    loads[2].wait()
    loads[3].wait()
    lax.fori_loop(0, CHUNKS, chunk, 0)

    mean = ssq[...].sum(-1, keepdims=True) * (1.0 / width)
    rs_all[slot] = jnp.broadcast_to(lax.rsqrt(mean + 1e-05), ssq.shape)

    def rs_copy(e, other):
        device = at(x, z, turn(y, e), 1 - core if other else core)
        return remote(
            rs_all.at[slot], rs_all.at[slot], rss_sem.at[other, e], rsr_sem.at[slot], device
        )

    def rs_arrival(e, other):
        s = (1 - core if other else core) * RING + turn(y, e)
        return remote(
            rs_all.at[s], rs_all.at[s], rss_sem.at[other, e], rsr_sem.at[s], sibling
        )

    others = [(e, other) for other in range(2) for e in range(RING) if (e, other) != (0, 0)]
    for e, other in others:
        rs_copy(e, other).start()

    a_relay(1)
    relay(0)
    origin(1)
    for j in range(2):
        for e in range(1, RING):
            a_onward(j, e).wait_recv()
            a_onward(j, e).start()
    finish(0)
    for j in range(2):
        for y_at in range(RING):
            a_other(j, y_at).wait_recv()
    for e, other in others:
        rs_arrival(e, other).wait_recv()

    def part_copy(kind, e):
        part, got = ((kv_part, kv_got), (q_part, q_got))[kind]
        return remote(
            part.at[turn(z, e)], got.at[z], ps_sem.at[kind, e], pr_sem.at[kind, z], z_dev(e)
        )

    def part_arrival(kind, e):
        part, got = ((kv_part, kv_got), (q_part, q_got))[kind]
        source = turn(z, e)
        return remote(
            part.at[source], got.at[source], ps_sem.at[kind, e], pr_sem.at[kind, source], z_dev(e)
        )

    def project(kind):
        part = (kv_part, q_part)[kind]
        cols = (slice(q_width, None), slice(0, q_width))[kind]

        def one(m, carry):
            product = jnp.dot(
                a_full[sublanes(m * all_rows, all_rows), :], w_all[:, cols], preferred_element_type=F32
            ).astype(BF16)
            for i in range(2):
                for zz in range(RING):
                    first = (i * RING + zz) * own
                    part[zz, a_rows(m * 2 + i), :] = product[first : first + own]
            return carry

        lax.fori_loop(0, RING, one, 0)
        for e in range(1, RING):
            part_copy(kind, e).start()

    def part_sum(kind):
        part, got = ((kv_part, kv_got), (q_part, q_got))[kind]
        value = part[z].astype(F32)
        for e in range(1, RING):
            part_arrival(kind, e).wait_recv()
            value += got[turn(z, e)].astype(F32)
        return value

    project(0)
    project(1)
    relay(1)
    row_scale = jnp.concatenate([rs_all[s] for s in range(n_tp)], axis=0)[:, 0:1]
    kv_all[mine] = (part_sum(0) * row_scale).astype(BF16)

    def kv_copy(to):
        return remote(
            kv_all.at[mine], kv_all.at[mine], kvs_sem.at[to], kvr_sem.at[mine], group_dev(to)
        )

    def kv_arrival(source):
        return remote(
            kv_all.at[source], kv_all.at[source], kvs_sem.at[source], kvr_sem.at[source],
            group_dev(source),
        )

    partner = pair * 2 + 1 - x_hi

    def kv_send(to, carry):
        kv_copy(to).start()
        return carry

    kv_copy(partner).start()
    lax.fori_loop(pair * 2 + 2, n_ctx, kv_send, 0)
    q_rows = (part_sum(1) * row_scale).astype(BF16)
    for h in range(heads):
        q_all[h] = q_rows[:, h * HEAD : (h + 1) * HEAD]

    def attend(b, first, some):
        keys = jnp.concatenate([kv_all[2 * b, :, :HEAD], kv_all[2 * b + 1, :, :HEAD]], axis=0)
        values = jnp.concatenate([kv_all[2 * b, :, HEAD:], kv_all[2 * b + 1, :, HEAD:]], axis=0)
        for u in range(2):
            h = some * 2 + u
            s = lax.dot_general(
                q_all[h], keys, (((1,), (1,)), ((), ())), preferred_element_type=F32
            ) * (LOG2E * HEAD**-0.5)
            if first:
                run = all_rows // 2
                row = lax.broadcasted_iota(jnp.int32, s.shape, 0)
                col = lax.broadcasted_iota(jnp.int32, s.shape, 1)
                q_pos = row + x_hi * run + jnp.where(row >= run, run, 0)
                in_block = jnp.where(col >= all_rows, col - all_rows, col)
                k_pos = (
                    in_block + jnp.where(col >= all_rows, run, 0) + jnp.where(in_block >= run, run, 0)
                )
                s = jnp.where(k_pos <= q_pos, s, -1e30)
                new_top = s.max(-1, keepdims=True)
                p = jnp.exp2(s - new_top)
                total[h] = p.sum(-1, keepdims=True)
                mixed[h] = jnp.dot(p.astype(BF16), values, preferred_element_type=F32)
            else:
                old = top[h]
                new_top = jnp.maximum(old, s.max(-1, keepdims=True))
                scale = jnp.exp2(old - new_top)
                p = jnp.exp2(s - new_top)
                total[h] = total[h] * scale + p.sum(-1, keepdims=True)
                mixed[h] = mixed[h] * scale + jnp.dot(
                    p.astype(BF16), values, preferred_element_type=F32
                )
            top[h] = new_top

    def h_piece(some, source):
        return h_all.at[source, :, lanes(some * 2 * HEAD, 2 * HEAD)]

    def h_copy(some, e):
        return remote(
            h_piece(some, z), h_piece(some, z), hzs_sem.at[some, e], hzr_sem.at[some, z], z_dev(e)
        )

    def h_arrival(some, e):
        source = turn(z, e)
        return remote(
            h_piece(some, source), h_piece(some, source),
            hzs_sem.at[some, e], hzr_sem.at[some, source], z_dev(e),
        )

    kv_arrival(partner).wait_recv()

    def some_heads(some, carry):
        attend(pair, True, some)

        def earlier(b, carry):
            @pl.when(some == 0)
            def _():
                kv_arrival(2 * b).wait_recv()
                kv_arrival(2 * b + 1).wait_recv()

            attend(b, False, some)
            return carry

        lax.fori_loop(0, pair, earlier, 0)
        for u in range(2):
            h = some * 2 + u
            h_all[z, :, lanes(h * HEAD, HEAD)] = (mixed[h] / total[h]).astype(BF16)
        for e in range(1, RING):
            h_copy(some, e).start()
        return carry

    lax.fori_loop(0, heads // 2, some_heads, 0)

    finish(1)
    for some in range(heads // 2):
        for e in range(1, RING):
            h_arrival(some, e).wait_recv()

    cols_out = wo_all.shape[2]

    def out_cols(g):
        return lanes(g * cols_out, cols_out)

    def s_copy(g):
        return remote(
            s_send.at[:, out_cols(g)], s_got.at[:, out_cols(g)], ss_sem.at[g], sr_sem.at[g], sibling
        )

    def multiply(g, carry):
        for zz in range(RING):
            product = jnp.dot(h_all[zz], wo_all[g], preferred_element_type=F32)
            low, high = product[: all_rows // 2], product[all_rows // 2 :]
            stays = jnp.where(core == 0, low, high).astype(BF16)
            goes = jnp.where(core == 0, high, low).astype(BF16)
            for yy in range(RING):
                at_rows = a_rows(yy * RING + zz)
                keep[at_rows, out_cols(g)] = stays[yy * own : (yy + 1) * own]
                s_send[at_rows, out_cols(g)] = goes[yy * own : (yy + 1) * own]
        s_copy(g).start()
        return carry

    lax.fori_loop(0, SLOTS, multiply, 0)

    def y_rows(y_at):
        return sublanes(y_at * block_rows, block_rows)

    def y_copy(g, e):
        return remote(
            y_send.at[y_rows(turn(y, e)), out_cols(g)], y_got.at[y_rows(y), out_cols(g)],
            ys_sem.at[g, e], yr_sem.at[g, y], y_dev(e),
        )

    def y_arrival(g, e):
        source = turn(y, e)
        return remote(
            y_send.at[y_rows(source), out_cols(g)], y_got.at[y_rows(source), out_cols(g)],
            ys_sem.at[g, e], yr_sem.at[g, source], y_dev(e),
        )

    def reduce_cores(g, carry):
        where = out_cols(g)
        s_copy(g).wait_recv()
        y_send[:, where] = (keep[:, where].astype(F32) + s_got[:, where].astype(F32)).astype(BF16)
        for e in range(1, RING):
            y_copy(g, e).start()
        ring_sum[:, where] = (
            keep[y_rows(y), where].astype(F32) + s_got[y_rows(y), where].astype(F32)
        )
        return carry

    lax.fori_loop(0, SLOTS, reduce_cores, 0)

    def z_copy(g, e):
        return remote(
            z_send.at[a_rows(turn(z, e)), out_cols(g)], z_got.at[a_rows(z), out_cols(g)],
            zs_sem.at[g, e], zr_sem.at[g, z], z_dev(e),
        )

    def z_arrival(g, e):
        source = turn(z, e)
        return remote(
            z_send.at[a_rows(source), out_cols(g)], z_got.at[a_rows(source), out_cols(g)],
            zs_sem.at[g, e], zr_sem.at[g, source], z_dev(e),
        )

    def full_cols(g, z_at):
        return lanes(((g // 2) * n_tp + z_at * 2 + lax.rem(g, 2)) * cols_out, cols_out)

    def reduce_ring(g, carry):
        where = out_cols(g)
        for e in range(1, RING):
            y_arrival(g, e).wait_recv()
        value = ring_sum[:, where]
        for e in range(1, RING):
            value += y_got[y_rows(turn(y, e)), where].astype(F32)
        ring_sum[:, where] = value
        z_send[:, where] = value.astype(BF16)
        for e in range(1, RING):
            z_copy(g, e).start()
        pooled_v[:, full_cols(g, z)] += ring_sum[a_rows(z), where]
        return carry

    lax.fori_loop(0, SLOTS, reduce_ring, 0)

    def last(g):
        return remote(
            last_send.at[g], last_got.at[g], l_sem.at[0, g], l_sem.at[1, g], along(1)
        )

    def result(h):
        return pltpu.make_async_copy(
            stream.at[h], out_hbm.at[:, lanes(h * HEAD, HEAD)], o_sem.at[h]
        )

    def combine(g):
        last(g).wait_recv()
        for zz in range(RING):
            where = full_cols(g, zz)
            shifted[1:own, where] = pooled_v[0 : own - 1, where]
            shifted[0:1, where] = jnp.where(me == 0, 0.0, last_got[g, zz : zz + 1, :])
            for u in range(cols_out // HEAD):
                h = ((g // 2) * n_tp + zz * 2 + lax.rem(g, 2)) * (cols_out // HEAD) + u
                cols = lanes(h * HEAD, HEAD)
                add = shifted[:, cols]
                for j in range(POOL):
                    rows_j = pl.ds(j, own, stride=POOL)
                    stream[h, rows_j, :] = stream[h, rows_j, :] + up_ref[j : j + 1, cols] * add
                result(h).start()

    last_send[...] = jnp.zeros_like(last_send)

    def take_home(g, carry):
        @pl.when(g < SLOTS)
        def _():
            for e in range(1, RING):
                z_arrival(g, e).wait_recv()
                source = turn(z, e)
                pooled_v[:, full_cols(g, source)] += z_got[a_rows(source), out_cols(g)].astype(F32)
            for zz in range(RING):
                last_send[g, zz : zz + 1, :] = pooled_v[own - 1 : own, full_cols(g, zz)]
            last(g).start()

        @pl.when(g > 0)
        def _():
            combine(g - 1)

        return carry

    lax.fori_loop(0, SLOTS + 1, take_home, 0)

    for hc in range(CHUNKS):
        for which in range(2):
            halo_far(which, hc).wait_send()
            for e in range(1, RING):
                halo_near(which, hc, e).wait_send()

    @pl.when(jnp.logical_not(is_home))
    def _():
        for i in range(4):
            hand_over(i).wait_send()

    settle(0)
    settle(1)

    def a_settle(hc, carry):
        for p in range(2):

            @pl.when(lax.rem(hc, 2) * 2 + p != z)
            def _():
                a_z_copy(hc, p).wait_send()

        return carry

    lax.fori_loop(0, CHUNKS, a_settle, 0)
    for j in range(2):
        for e in range(RING):
            a_copy(j, e).wait_send()
        for e in range(1, RING):
            a_onward(j, e).wait_send()
    for e in range(1, RING):
        part_copy(0, e).wait_send()
        part_copy(1, e).wait_send()
        for some in range(heads // 2):
            h_copy(some, e).wait_send()
    for e, other in others:
        rs_copy(e, other).wait_send()

    def kv_settle(to, carry):
        kv_copy(to).wait_send()
        return carry

    kv_copy(partner).wait_send()
    lax.fori_loop(pair * 2 + 2, n_ctx, kv_settle, 0)

    def sums_settle(g, carry):
        s_copy(g).wait_send()
        for e in range(1, RING):
            y_copy(g, e).wait_send()
            z_copy(g, e).wait_send()
        last(g).wait_send()
        return carry

    lax.fori_loop(0, SLOTS, sums_settle, 0)

    def out_settle(h, carry):
        result(h).wait()
        return carry

    lax.fori_loop(0, width // HEAD, out_settle, 0)


def per_device(
    mesh, fine_x, fine_q, fine_k, fine_v, windows, pool_w, norm_gain, w_query, w_key, w_value, w_out, up_w
):
    rows, width = fine_q.shape
    kv_width = fine_k.shape[1]
    n_tp, n_ctx = mesh.shape["tp"], mesh.shape["ctx"]
    reach = WIN // rows
    span = (reach + 1) * rows
    own = rows // POOL
    all_rows = own * n_tp
    depth, q_width = w_query.shape
    heads = q_width // HEAD
    w_cols = q_width + 2 * HEAD
    dma = pltpu.SemaphoreType.DMA
    return pl.pallas_call(
        block_kernel,
        out_shape=jax.ShapeDtypeStruct((rows, width), F32),
        in_specs=[ANY_SPEC] * 4
        + [pl.BlockSpec(memory_space=pltpu.SMEM)]
        + [VMEM_SPEC] * 3
        + [ANY_SPEC] * 4,
        out_specs=ANY_SPEC,
        scratch_shapes=[
            pltpu.VMEM((rows, width), BF16),
            pltpu.VMEM((rows, width), BF16),
            pltpu.VMEM((span, kv_width), BF16),
            pltpu.VMEM((span, kv_width), BF16),
            pltpu.VMEM((rows, span), jnp.int32),
            pltpu.VMEM((width // HEAD, rows, HEAD), F32),
            pltpu.VMEM((own, width), F32),
            pltpu.VMEM((own, width), BF16),
            pltpu.VMEM((RING * all_rows, width // RING), BF16),
            pltpu.VMEM((n_tp, own, HEAD), F32),
            pltpu.VMEM((own, HEAD), F32),
            pltpu.VMEM((SLOTS * depth, w_cols), BF16),
            pltpu.VMEM((SLOTS,) + w_out.shape, BF16),
            pltpu.VMEM((RING, all_rows, 2 * HEAD), BF16),
            pltpu.VMEM((RING, all_rows, q_width), BF16),
            pltpu.VMEM((RING, all_rows, 2 * HEAD), BF16),
            pltpu.VMEM((RING, all_rows, q_width), BF16),
            pltpu.VMEM((n_ctx, all_rows, 2 * HEAD), BF16),
            pltpu.VMEM((heads, all_rows, HEAD), BF16),
            pltpu.VMEM((heads, all_rows, 1), F32),
            pltpu.VMEM((heads, all_rows, 1), F32),
            pltpu.VMEM((heads, all_rows, HEAD), F32),
            pltpu.VMEM((RING, all_rows, q_width), BF16),
        ]
        + [pltpu.VMEM((RING * all_rows // 2, width // RING), BF16)] * 5
        + [
            pltpu.VMEM((RING * own, width // RING), F32),
            pltpu.VMEM((RING * own, width // RING), BF16),
            pltpu.VMEM((RING * own, width // RING), BF16),
            pltpu.VMEM((own, width), F32),
            pltpu.VMEM((SLOTS, 8, w_out.shape[1]), F32),
            pltpu.VMEM((SLOTS, 8, w_out.shape[1]), F32),
            dma((4,)),
            dma((2, CHUNKS, reach)),
            dma((2, CHUNKS, reach)),
            dma((CHUNKS, 2)),
            dma((2, RING)),
            dma((2, RING)),
            dma((2, n_tp)),
            dma((2, RING)),
            dma((2, RING)),
            dma((n_tp,)),
            dma((3, 4)),
            dma((2, SLOTS, 2)),
            dma((2, SLOTS)),
            dma((2, RING)),
            dma((2, RING)),
            dma((n_ctx,)),
            dma((n_ctx,)),
            dma((heads // 2, RING)),
            dma((heads // 2, RING)),
            dma((SLOTS,)),
            dma((SLOTS,)),
            dma((SLOTS, RING)),
            dma((SLOTS, RING)),
            dma((SLOTS, RING)),
            dma((SLOTS, RING)),
            dma((2, SLOTS)),
            dma((width // HEAD,)),
        ],
        compiler_params=pltpu.CompilerParams(
            collective_id=0, has_side_effects=True, vmem_limit_bytes=62 * 2**20
        ),
        name="hourglass",
    )(
        fine_q, fine_k, fine_v, fine_x, windows, pool_w, norm_gain[None], up_w,
        w_query, w_key, w_value, w_out,
    )


def solution(mesh):
    placed = (
        P(("ctx", "tp"), None),
        P(("ctx", "tp"), None),
        P(("ctx", "tp"), None),
        P(("ctx", "tp"), None),
        P(),
        P(),
        P(),
        P("ctx", "tp"),
        P("ctx", "tp"),
        P("ctx", "tp"),
        P("tp", "ctx"),
        P(),
    )
    return jax.shard_map(
        functools.partial(per_device, mesh),
        mesh=mesh,
        in_specs=placed,
        out_specs=P(("ctx", "tp"), None),
        check_vma=False,
    )
```

```python
import functools

import jax
import jax.numpy as jnp
from jax import lax
from jax.experimental import pallas as pl
from jax.experimental.pallas import tpu as pltpu
from jax.sharding import PartitionSpec as P

HEAD = 128
WIN = 512
POOL = 4
RING = 4
LOG2E = 1.4426950408889634
MESH = pl.DeviceIdType.MESH
F32 = jnp.float32
BF16 = jnp.bfloat16
VMEM_SPEC = pl.BlockSpec(memory_space=pltpu.VMEM)
ANY_SPEC = pl.BlockSpec(memory_space=pl.ANY)
CHUNKS = 4
SLOTS = 4


def lanes(start, size):
    return pl.ds(pl.multiple_of(start, 128), size)


def sublanes(start, size):
    return pl.ds(pl.multiple_of(start, size), size)


def block_kernel(
    q_hbm, k_hbm, v_hbm, x_hbm, win_ref, pw_ref, gain_ref, up_ref, wq_hbm, wk_hbm, wv_hbm, wo_hbm,
    out_hbm,
    q_ref, x_ref, kbuf, vbuf, dist, stream, pooled_v, a_own, a_full, rs_all, ssq,
    w_all, wo_all, part, part_got, kv_all, q_all, top, total, mixed, h_all,
    keep, s_send, s_got, y_send, y_got, ring_sum, z_send, z_got, shifted, last_send, last_got,
    in_sem, hs_sem, hr_sem, azs_sem, azr_sem, ays_sem, ayr_sem, acs_sem, aps_sem, apr_sem, rss_sem, rsr_sem,
    ho_sem, wgs_sem, wgr_sem, ps_sem, pr_sem, k1s_sem, k2s_sem, v1s_sem, v2s_sem, kr_sem, vr_sem, hzs_sem, hzr_sem,
    ss_sem, sr_sem, ys_sem, yr_sem, zs_sem, zr_sem, l_sem, o_sem,
):
    rows, width = q_ref.shape
    kv_width = kbuf.shape[1]
    reach = WIN // rows
    span = (reach + 1) * rows
    group = width // kv_width
    own = rows // POOL
    kv_chunk = kv_width // CHUNKS
    q_chunk = width // CHUNKS
    depth = w_all.shape[0] // SLOTS
    q_width = h_all.shape[2]
    heads = q_width // HEAD
    all_rows = h_all.shape[1]
    n_tp = 2 * RING
    n_ctx = 4 * RING
    n_dev = n_ctx * n_tp

    ctx = lax.axis_index("ctx")
    tp = lax.axis_index("tp")
    me = ctx * n_tp + tp
    x_lo = ctx // n_tp
    z = lax.rem(ctx, n_tp) // 2
    core = lax.rem(ctx, 2)
    x_hi = tp // RING
    y = lax.rem(tp, RING)
    x = 2 * x_hi + x_lo
    pair = x_lo * RING + z
    mine = pair * 2 + x_hi
    slot = core * RING + y

    def at(x_at, z_at, y_at, core_at):
        return (lax.rem(x_at, 2) * n_tp + z_at * 2 + core_at, (x_at // 2) * RING + y_at)

    def along(step):
        other = lax.rem(me + step + n_dev, n_dev)
        return (other // n_tp, lax.rem(other, n_tp))

    def turn(value, step):
        return lax.rem(value + step + 2 * RING, RING)

    def y_dev(step):
        return at(x, z, turn(y, step), core)

    def z_dev(step):
        return at(x, turn(z, step), y, core)

    def group_dev(g):
        p = g // 2
        return at(2 * lax.rem(g, 2) + p // RING, lax.rem(p, RING), y, core)

    sibling = at(x, z, y, 1 - core)

    def remote(src, dst, send_sem, recv_sem, device):
        return pltpu.make_async_remote_copy(
            src_ref=src, dst_ref=dst, send_sem=send_sem, recv_sem=recv_sem,
            device_id=device, device_id_type=MESH,
        )

    last_rows = pl.ds(reach * rows, rows)
    loads = [
        pltpu.make_async_copy(src, dst, in_sem.at[i])
        for i, (src, dst) in enumerate(
            ((k_hbm, kbuf.at[last_rows]), (v_hbm, vbuf.at[last_rows]), (q_hbm, q_ref), (x_hbm, x_ref))
        )
    ]
    for load in loads:
        load.start()
    barrier = pltpu.get_barrier_semaphore()

    def greet(device):
        pl.semaphore_signal(barrier, inc=1, device_id=device, device_id_type=MESH)

    for e in range(1, RING):
        greet(y_dev(e))
        greet(at(x, z, turn(y, e), 1 - core))
    greet(sibling)
    greet(along(-reach))
    greet(along(-1))

    def greet_plane(d, carry):
        greet(group_dev(lax.rem(mine + d, n_ctx)))
        return carry

    lax.fori_loop(1, n_ctx, greet_plane, 0)
    pl.semaphore_wait(barrier, 2 * RING + 1 + n_ctx - 1)

    def block_cols(hc):
        return lanes(hc * kv_chunk, kv_chunk)

    def halo_copy(which, hc, d, device, source):
        buf = (kbuf, vbuf)[which]
        return remote(
            buf.at[sublanes(source * rows, rows), block_cols(hc)],
            buf.at[pl.ds((reach - d) * rows, rows), block_cols(hc)],
            hs_sem.at[which, hc, d - 1],
            hr_sem.at[which, hc, d - 1],
            device,
        )

    def halo_far(which, hc):
        return halo_copy(which, hc, reach, along(reach), reach)

    def halo_near(which, hc, e):
        return halo_copy(which, hc, e, y_dev(e), jnp.where(y + e < RING, reach, 0))

    loads[0].wait()
    loads[1].wait()
    for hc in range(2):
        for which in range(2):
            halo_far(which, hc).start()

    is_home = core == x_hi

    def shard_parts(core_at):
        to = x_lo * 2 + core_at
        rows_to = sublanes(to * depth, depth)
        return (
            (wq_hbm, w_all.at[rows_to, 0:q_width]),
            (wk_hbm, w_all.at[rows_to, q_width : q_width + HEAD]),
            (wv_hbm, w_all.at[rows_to, q_width + HEAD : q_width + 2 * HEAD]),
            (wo_hbm, wo_all.at[to]),
        )

    def hand_over(i):
        src, dst = shard_parts(core)[i]
        return remote(src, dst, ho_sem.at[0, i], ho_sem.at[1, i], sibling)

    def hand_over_arrival(i):
        src, dst = shard_parts(1 - core)[i]
        return remote(src, dst, ho_sem.at[0, i], ho_sem.at[1, i], sibling)

    def stay(i):
        src, dst = shard_parts(core)[i]
        return pltpu.make_async_copy(src, dst, ho_sem.at[2, i])

    @pl.when(is_home)
    def _():
        for i in range(4):
            stay(i).start()

    @pl.when(jnp.logical_not(is_home))
    def _():
        for i in range(4):
            hand_over(i).start()

    for hc in range(2):
        for which in range(2):
            for e in range(1, RING):

                @pl.when(y + e < RING)
                def _():
                    halo_near(which, hc, e).start()

    def hop(kind, k, lane):
        piece = w_all.at[sublanes(k * depth, depth)] if kind == 0 else wo_all.at[k]
        device = at(turn(x, 1 if lane == 0 else -1), z, y, core)
        return remote(piece, piece, wgs_sem.at[kind, k, lane], wgr_sem.at[kind, k], device)

    def off_x(k):
        return turn(x, -2 * core - k // 2)

    def hop_wanted(k, lane):
        onward = (off_x(k) == 1) & (lax.rem(k, 2) == 0)
        back = (off_x(k) == 3) & (lax.rem(k, 2) == 1)
        return (off_x(k) == 0) | (onward if lane == 0 else back)

    def launch(kind, k):
        for lane in range(2):

            @pl.when(hop_wanted(k, lane))
            def _():
                hop(kind, k, lane).start()

    def origin(kind):
        @pl.when(is_home)
        def _():
            for i in range(4):
                if (i == 3) == (kind == 1):
                    stay(i).wait()
                    hand_over_arrival(i).wait_recv()
            for c in range(2):
                launch(kind, x_lo * 2 + c)

    def relay(kind):
        def one(k, carry):
            @pl.when((off_x(k) == 1) | (off_x(k) == 3))
            def _():
                hop(kind, k, 0).wait_recv()
                launch(kind, k)

            return carry

        lax.fori_loop(0, SLOTS, one, 0)

    def finish(kind):
        def one(k, carry):
            @pl.when(off_x(k) == 2)
            def _():
                hop(kind, k, 0).wait_recv()

            return carry

        lax.fori_loop(0, SLOTS, one, 0)

    def settle(kind):
        def one(k, carry):
            for lane in range(2):

                @pl.when(hop_wanted(k, lane))
                def _():
                    hop(kind, k, lane).wait_send()

            return carry

        lax.fori_loop(0, SLOTS, one, 0)

    for hc in range(2):
        for which in range(2):
            halo_far(which, hc).wait_recv()
            halo_far(which, hc + 2).start()
        for which in range(2):
            for e in range(1, RING):

                @pl.when(y + e >= RING)
                def _():
                    halo_near(which, hc, e).start()

    origin(0)
    q_at = lax.broadcasted_iota(jnp.int32, (rows, span), 0)
    l_at = lax.broadcasted_iota(jnp.int32, (rows, span), 1)
    gap = reach * rows + q_at - l_at
    outside = (gap < 0) | (l_at < (reach - me) * rows)
    dist[...] = jnp.where(outside, 2 * span, gap)
    ssq[...] = jnp.zeros_like(ssq)

    def a_rows(s):
        return sublanes(s * own, own)

    piece_cols = q_chunk // 2
    block_rows = RING * own

    def a_z_copy(hc, p):
        to = lax.rem(hc, 2) * 2 + p
        return remote(
            a_own.at[:, lanes(hc * q_chunk + p * piece_cols, piece_cols)],
            a_full.at[a_rows(slot * RING + z), lanes((hc // 2) * piece_cols, piece_cols)],
            azs_sem.at[hc, p],
            azr_sem.at[hc // 2, z],
            at(x, to, y, core),
        )

    def a_z_arrival(j, e):
        source = turn(z, e)
        piece = a_full.at[a_rows(slot * RING + source), lanes(j * piece_cols, piece_cols)]
        return remote(piece, piece, azs_sem.at[0, 0], azr_sem.at[j, source], z_dev(e))

    def a_block(j, s):
        return a_full.at[sublanes(s * block_rows, block_rows), lanes(j * piece_cols, piece_cols)]

    def a_copy(j, e):
        device = sibling if e == 0 else y_dev(e)
        return remote(
            a_block(j, slot), a_block(j, slot), ays_sem.at[j, e], ayr_sem.at[j, slot], device
        )

    def a_onward(j, e):
        s = core * RING + turn(y, -e)
        return remote(a_block(j, s), a_block(j, s), acs_sem.at[j, e], ayr_sem.at[j, s], sibling)

    def a_other(j, y_at):
        s = (1 - core) * RING + y_at
        return remote(a_block(j, s), a_block(j, s), acs_sem.at[j, 0], ayr_sem.at[j, s], sibling)

    def a_relay(j):
        for e in range(1, RING):
            a_z_arrival(j, e).wait_recv()
        for e in (1, 3, 0):
            a_copy(j, e).start()

    def a_pass(j, side):
        s = core * RING + turn(y, -1 if side == 0 else 1)
        part_rows = block_rows // 2
        piece = a_full.at[
            sublanes((2 * s + side) * part_rows, part_rows), lanes(j * piece_cols, piece_cols)
        ]
        return remote(
            piece, piece, aps_sem.at[j, side], apr_sem.at[j, side], y_dev(1 if side == 0 else -1)
        )

    def a_passed(j, side):
        s = core * RING + turn(y, 2)
        part_rows = block_rows // 2
        piece = a_full.at[
            sublanes((2 * s + side) * part_rows, part_rows), lanes(j * piece_cols, piece_cols)
        ]
        return remote(piece, piece, aps_sem.at[j, side], apr_sem.at[j, side], y_dev(2))

    part_heads = group // 2

    def chunk(hc, carry):
        for which in range(2):
            for e in range(1, RING):
                halo_near(which, hc, e).wait_recv()

        @pl.when(hc < CHUNKS - 2)
        def _():
            for which in range(2):
                halo_far(which, hc + 2).wait_recv()
                for e in range(1, RING):
                    halo_near(which, hc + 2, e).start()

        for u in range(kv_chunk // HEAD):
            kv_cols = lanes(hc * kv_chunk + u * HEAD, HEAD)
            keys = kbuf[:, kv_cols]
            values = vbuf[:, kv_cols]
            for part in range(2):
                first = (hc * (kv_chunk // HEAD) + u) * group + part * part_heads
                qs = jnp.concatenate(
                    [q_ref[:, lanes((first + i) * HEAD, HEAD)] for i in range(part_heads)], axis=0
                )
                scores = lax.dot_general(
                    qs, keys, (((1,), (1,)), ((), ())), preferred_element_type=F32
                )
                weights, totals = [], []
                for i in range(part_heads):
                    s = scores[i * rows : (i + 1) * rows] * (LOG2E * HEAD**-0.5)
                    s = jnp.where(dist[...] < win_ref[first + i], s, -1e30)
                    p = jnp.exp2(s - s.max(-1, keepdims=True))
                    totals.append(p.sum(-1, keepdims=True))
                    weights.append(p.astype(BF16))
                out = jnp.dot(
                    jnp.concatenate(weights, axis=0), values, preferred_element_type=F32
                )
                for i in range(part_heads):
                    cols = lanes((first + i) * HEAD, HEAD)
                    stream[first + i] = (
                        x_ref[:, cols].astype(F32) + out[i * rows : (i + 1) * rows] / totals[i]
                    )
        for i in range(q_chunk // HEAD):
            cols = lanes(hc * q_chunk + i * HEAD, HEAD)
            head = hc * (q_chunk // HEAD) + i
            pooled = sum(
                pw_ref[j : j + 1, cols] * stream[head, pl.ds(j, own, stride=POOL), :]
                for j in range(POOL)
            )
            pooled_v[:, cols] = pooled
            ssq[...] += pooled * pooled
            a_own[:, cols] = (pooled * gain_ref[:, cols]).astype(BF16)
        for p in range(2):
            to = lax.rem(hc, 2) * 2 + p

            @pl.when(to != z)
            def _():
                a_z_copy(hc, p).start()

            @pl.when(to == z)
            def _():
                a_full[a_rows(slot * RING + z), lanes((hc // 2) * piece_cols, piece_cols)] = a_own[
                    :, lanes(hc * q_chunk + p * piece_cols, piece_cols)
                ]

        @pl.when(hc == 2)
        def _():
            a_relay(0)

        return carry

    loads[2].wait()
    loads[3].wait()
    lax.fori_loop(0, CHUNKS, chunk, 0)

    mean = ssq[...].sum(-1, keepdims=True) * (1.0 / width)
    rs_all[slot] = jnp.broadcast_to(lax.rsqrt(mean + 1e-05), ssq.shape)

    def rs_copy(e, other):
        device = at(x, z, turn(y, e), 1 - core if other else core)
        return remote(
            rs_all.at[slot], rs_all.at[slot], rss_sem.at[other, e], rsr_sem.at[slot], device
        )

    def rs_arrival(e, other):
        s = (1 - core if other else core) * RING + turn(y, e)
        return remote(
            rs_all.at[s], rs_all.at[s], rss_sem.at[other, e], rsr_sem.at[s], sibling
        )

    others = [(e, other) for other in range(2) for e in range(RING) if (e, other) != (0, 0)]
    for e, other in others:
        rs_copy(e, other).start()

    a_relay(1)
    for j in range(2):
        for side, e in enumerate((1, 3)):
            a_onward(j, e).wait_recv()
            a_pass(j, side).start()
            a_onward(j, e).start()
        if j == 0:
            relay(0)
    for j in range(2):
        a_passed(j, 0).wait_recv()
        a_passed(j, 1).wait_recv()
        a_onward(j, 2).start()
    finish(0)
    origin(1)
    for j in range(2):
        for y_at in range(RING):
            a_other(j, y_at).wait_recv()
    for e, other in others:
        rs_arrival(e, other).wait_recv()

    def part_copy(kind, e):
        return remote(
            part.at[kind, turn(z, e)], part_got.at[kind, z],
            ps_sem.at[kind, e], pr_sem.at[kind, z], z_dev(e),
        )

    def part_arrival(kind, e):
        source = turn(z, e)
        return remote(
            part.at[kind, source], part_got.at[kind, source],
            ps_sem.at[kind, e], pr_sem.at[kind, source], z_dev(e),
        )

    two_heads = 2 * HEAD

    def project(kind):
        first_col = (q_width, 0, two_heads)[kind]
        cols = slice(first_col, first_col + two_heads)

        def one(m, carry):
            product = jnp.dot(
                a_full[sublanes(m * all_rows, all_rows), :], w_all[:, cols], preferred_element_type=F32
            ).astype(BF16)
            for i in range(2):
                for zz in range(RING):
                    first = (i * RING + zz) * own
                    part[kind, zz, a_rows(m * 2 + i), :] = product[first : first + own]
            return carry

        lax.fori_loop(0, RING, one, 0)
        for e in range(1, RING):
            part_copy(kind, e).start()

    def part_sum(kind):
        value = part[kind, z].astype(F32)
        for e in range(1, RING):
            part_arrival(kind, e).wait_recv()
            value += part_got[kind, turn(z, e)].astype(F32)
        return value

    project(0)
    project(1)
    row_scale = jnp.concatenate([rs_all[s] for s in range(n_tp)], axis=0)[:, 0:1]
    kv_all[mine] = (part_sum(0) * row_scale).astype(BF16)

    def home(x_at, z_at):
        return (lax.rem(x_at, 2) * RING + z_at) * 2 + x_at // 2

    def key_of(g):
        return kv_all.at[g, :, 0:HEAD]

    def value_of(g):
        return kv_all.at[g, :, HEAD : 2 * HEAD]

    def key_x(e):
        to = turn(x, e)
        copy = remote(key_of(mine), key_of(mine), k1s_sem.at[e], kr_sem.at[mine], at(to, z, y, core))
        return copy, lax.rem(to, 2) >= x_lo

    def key_z(x_at, e):
        to, g, lo = turn(z, e), home(x_at, z), lax.rem(x_at, 2)
        copy = remote(key_of(g), key_of(g), k2s_sem.at[x_at, e], kr_sem.at[g], at(x, to, y, core))
        return copy, (lo < x_lo) | ((lo == x_lo) & (to > z))

    def value_z(e):
        to = turn(z, e)
        copy = remote(
            value_of(mine), value_of(mine), v1s_sem.at[e], vr_sem.at[mine], at(x, to, y, core)
        )
        return copy, (x_lo == 0) | (to > z)

    def value_x(z_at, e):
        to, g = turn(x, e), home(x, z_at)
        lo = lax.rem(to, 2)
        copy = remote(value_of(g), value_of(g), v2s_sem.at[z_at, e], vr_sem.at[g], at(to, z, y, core))
        return copy, (lo > x_lo) | ((lo == x_lo) & (z_at <= z))

    def key_arrival(g):
        return remote(key_of(g), key_of(g), k1s_sem.at[0], kr_sem.at[g], sibling)

    def value_arrival(g):
        return remote(value_of(g), value_of(g), v1s_sem.at[0], vr_sem.at[g], sibling)

    def begin(copy_and_wanted):
        copy, wanted = copy_and_wanted

        @pl.when(wanted)
        def _():
            copy.start()

    def end(copy_and_wanted):
        copy, wanted = copy_and_wanted

        @pl.when(wanted)
        def _():
            copy.wait_send()

    for e in range(1, RING):
        begin(key_x(e))
        begin(value_z(e))
    for e in range(1, RING):
        begin(value_x(z, e))
        begin(key_z(x, e))

    def kv_relay(e, carry):
        x_at, z_at = turn(x, e), turn(z, e)

        @pl.when(lax.rem(x_at, 2) <= x_lo)
        def _():
            key_arrival(home(x_at, z)).wait_recv()
            for e2 in range(1, RING):
                begin(key_z(x_at, e2))

        @pl.when((x_lo == 0) | (z_at < z))
        def _():
            value_arrival(home(x, z_at)).wait_recv()
            for e2 in range(1, RING):
                begin(value_x(z_at, e2))

        return carry

    lax.fori_loop(1, RING, kv_relay, 0)
    partner = pair * 2 + 1 - x_hi
    project(2)
    relay(1)

    def take_queries(some):
        scale = jnp.concatenate([rs_all[s] for s in range(n_tp)], axis=0)[:, 0:1]
        q_rows = (part_sum(1 + some) * scale).astype(BF16)
        for u in range(2):
            q_all[some * 2 + u] = q_rows[:, u * HEAD : (u + 1) * HEAD]

    take_queries(0)

    def attend(b, first, some):
        keys = jnp.concatenate([kv_all[2 * b, :, :HEAD], kv_all[2 * b + 1, :, :HEAD]], axis=0)
        values = jnp.concatenate([kv_all[2 * b, :, HEAD:], kv_all[2 * b + 1, :, HEAD:]], axis=0)
        for u in range(2):
            h = some * 2 + u
            s = lax.dot_general(
                q_all[h], keys, (((1,), (1,)), ((), ())), preferred_element_type=F32
            ) * (LOG2E * HEAD**-0.5)
            if first:
                run = all_rows // 2
                row = lax.broadcasted_iota(jnp.int32, s.shape, 0)
                col = lax.broadcasted_iota(jnp.int32, s.shape, 1)
                q_pos = row + x_hi * run + jnp.where(row >= run, run, 0)
                in_block = jnp.where(col >= all_rows, col - all_rows, col)
                k_pos = (
                    in_block + jnp.where(col >= all_rows, run, 0) + jnp.where(in_block >= run, run, 0)
                )
                s = jnp.where(k_pos <= q_pos, s, -1e30)
                new_top = s.max(-1, keepdims=True)
                p = jnp.exp2(s - new_top)
                total[h] = p.sum(-1, keepdims=True)
                mixed[h] = jnp.dot(p.astype(BF16), values, preferred_element_type=F32)
            else:
                old = top[h]
                new_top = jnp.maximum(old, s.max(-1, keepdims=True))
                scale = jnp.exp2(old - new_top)
                p = jnp.exp2(s - new_top)
                total[h] = total[h] * scale + p.sum(-1, keepdims=True)
                mixed[h] = mixed[h] * scale + jnp.dot(
                    p.astype(BF16), values, preferred_element_type=F32
                )
            top[h] = new_top

    def h_piece(some, source):
        return h_all.at[source, :, lanes(some * 2 * HEAD, 2 * HEAD)]

    def h_copy(some, e):
        return remote(
            h_piece(some, z), h_piece(some, z), hzs_sem.at[some, e], hzr_sem.at[some, z], z_dev(e)
        )

    def h_arrival(some, e):
        source = turn(z, e)
        return remote(
            h_piece(some, source), h_piece(some, source),
            hzs_sem.at[some, e], hzr_sem.at[some, source], z_dev(e),
        )

    value_arrival(partner).wait_recv()

    def some_heads(some, carry):
        @pl.when(some == 1)
        def _():
            take_queries(1)

        attend(pair, True, some)

        def earlier(b, carry):
            @pl.when(some == 0)
            def _():
                @pl.when(lax.rem(b, RING) != z)
                def _():
                    key_arrival(2 * b).wait_recv()
                    key_arrival(2 * b + 1).wait_recv()

                for hi in range(2):

                    @pl.when(2 * hi + b // RING != x)
                    def _():
                        value_arrival(2 * b + hi).wait_recv()

            attend(b, False, some)
            return carry

        lax.fori_loop(0, pair, earlier, 0)
        for u in range(2):
            h = some * 2 + u
            h_all[z, :, lanes(h * HEAD, HEAD)] = (mixed[h] / total[h]).astype(BF16)
        for e in range(1, RING):
            h_copy(some, e).start()
        return carry

    lax.fori_loop(0, heads // 2, some_heads, 0)

    finish(1)
    for some in range(heads // 2):
        for e in range(1, RING):
            h_arrival(some, e).wait_recv()

    cols_out = wo_all.shape[2]

    def out_cols(g):
        return lanes(g * cols_out, cols_out)

    def s_copy(g):
        return remote(
            s_send.at[:, out_cols(g)], s_got.at[:, out_cols(g)], ss_sem.at[g], sr_sem.at[g], sibling
        )

    def multiply(g, carry):
        for zz in range(RING):
            product = jnp.dot(h_all[zz], wo_all[g], preferred_element_type=F32)
            low, high = product[: all_rows // 2], product[all_rows // 2 :]
            stays = jnp.where(core == 0, low, high).astype(BF16)
            goes = jnp.where(core == 0, high, low).astype(BF16)
            for yy in range(RING):
                at_rows = a_rows(yy * RING + zz)
                keep[at_rows, out_cols(g)] = stays[yy * own : (yy + 1) * own]
                s_send[at_rows, out_cols(g)] = goes[yy * own : (yy + 1) * own]
        s_copy(g).start()
        return carry


    def y_rows(y_at):
        return sublanes(y_at * block_rows, block_rows)

    def y_copy(g, e):
        return remote(
            y_send.at[y_rows(turn(y, e)), out_cols(g)], y_got.at[y_rows(y), out_cols(g)],
            ys_sem.at[g, e], yr_sem.at[g, y], y_dev(e),
        )

    def y_arrival(g, e):
        source = turn(y, e)
        return remote(
            y_send.at[y_rows(source), out_cols(g)], y_got.at[y_rows(source), out_cols(g)],
            ys_sem.at[g, e], yr_sem.at[g, source], y_dev(e),
        )

    def reduce_cores(g, carry):
        where = out_cols(g)
        s_copy(g).wait_recv()
        y_send[:, where] = (keep[:, where].astype(F32) + s_got[:, where].astype(F32)).astype(BF16)
        for e in range(1, RING):
            y_copy(g, e).start()
        ring_sum[:, where] = (
            keep[y_rows(y), where].astype(F32) + s_got[y_rows(y), where].astype(F32)
        )
        return carry

    def sums(g, carry):
        @pl.when(g < SLOTS)
        def _():
            multiply(g, 0)

        @pl.when(g > 0)
        def _():
            reduce_cores(g - 1, 0)

        return carry

    lax.fori_loop(0, SLOTS + 1, sums, 0)

    def z_copy(g, e):
        return remote(
            z_send.at[a_rows(turn(z, e)), out_cols(g)], z_got.at[a_rows(z), out_cols(g)],
            zs_sem.at[g, e], zr_sem.at[g, z], z_dev(e),
        )

    def z_arrival(g, e):
        source = turn(z, e)
        return remote(
            z_send.at[a_rows(source), out_cols(g)], z_got.at[a_rows(source), out_cols(g)],
            zs_sem.at[g, e], zr_sem.at[g, source], z_dev(e),
        )

    def full_cols(g, z_at):
        return lanes(((g // 2) * n_tp + z_at * 2 + lax.rem(g, 2)) * cols_out, cols_out)

    def reduce_ring(g, carry):
        where = out_cols(g)
        for e in range(1, RING):
            y_arrival(g, e).wait_recv()
        value = ring_sum[:, where]
        for e in range(1, RING):
            value += y_got[y_rows(turn(y, e)), where].astype(F32)
        ring_sum[:, where] = value
        z_send[:, where] = value.astype(BF16)
        for e in range(1, RING):
            z_copy(g, e).start()
        pooled_v[:, full_cols(g, z)] += ring_sum[a_rows(z), where]
        return carry

    lax.fori_loop(0, SLOTS, reduce_ring, 0)

    def last(g):
        return remote(
            last_send.at[g], last_got.at[g], l_sem.at[0, g], l_sem.at[1, g], along(1)
        )

    def result(h):
        return pltpu.make_async_copy(
            stream.at[h], out_hbm.at[:, lanes(h * HEAD, HEAD)], o_sem.at[h]
        )

    def combine(g):
        last(g).wait_recv()
        for zz in range(RING):
            where = full_cols(g, zz)
            shifted[1:own, where] = pooled_v[0 : own - 1, where]
            shifted[0:1, where] = jnp.where(me == 0, 0.0, last_got[g, zz : zz + 1, :])
            for u in range(cols_out // HEAD):
                h = ((g // 2) * n_tp + zz * 2 + lax.rem(g, 2)) * (cols_out // HEAD) + u
                cols = lanes(h * HEAD, HEAD)
                add = shifted[:, cols]
                for j in range(POOL):
                    rows_j = pl.ds(j, own, stride=POOL)
                    stream[h, rows_j, :] = stream[h, rows_j, :] + up_ref[j : j + 1, cols] * add
                result(h).start()

    last_send[...] = jnp.zeros_like(last_send)

    def take_home(g, carry):
        @pl.when(g < SLOTS)
        def _():
            for e in range(1, RING):
                z_arrival(g, e).wait_recv()
                source = turn(z, e)
                pooled_v[:, full_cols(g, source)] += z_got[a_rows(source), out_cols(g)].astype(F32)
            for zz in range(RING):
                last_send[g, zz : zz + 1, :] = pooled_v[own - 1 : own, full_cols(g, zz)]
            last(g).start()

        @pl.when(g > 0)
        def _():
            combine(g - 1)

        return carry

    lax.fori_loop(0, SLOTS + 1, take_home, 0)

    for hc in range(CHUNKS):
        for which in range(2):
            halo_far(which, hc).wait_send()
            for e in range(1, RING):
                halo_near(which, hc, e).wait_send()

    @pl.when(jnp.logical_not(is_home))
    def _():
        for i in range(4):
            hand_over(i).wait_send()

    settle(0)
    settle(1)

    def a_settle(hc, carry):
        for p in range(2):

            @pl.when(lax.rem(hc, 2) * 2 + p != z)
            def _():
                a_z_copy(hc, p).wait_send()

        return carry

    lax.fori_loop(0, CHUNKS, a_settle, 0)
    for j in range(2):
        for e in (1, 3, 0):
            a_copy(j, e).wait_send()
        a_pass(j, 0).wait_send()
        a_pass(j, 1).wait_send()
        for e in range(1, RING):
            a_onward(j, e).wait_send()
    for e in range(1, RING):
        for kind in range(3):
            part_copy(kind, e).wait_send()
        for some in range(heads // 2):
            h_copy(some, e).wait_send()
    for e, other in others:
        rs_copy(e, other).wait_send()

    for e in range(1, RING):
        end(key_x(e))
        end(value_z(e))

    def kv_settle(i, carry):
        for e in range(1, RING):

            @pl.when(lax.rem(i, 2) <= x_lo)
            def _():
                end(key_z(i, e))

            @pl.when((x_lo == 0) | (i <= z))
            def _():
                end(value_x(i, e))

        return carry

    lax.fori_loop(0, RING, kv_settle, 0)

    def sums_settle(g, carry):
        s_copy(g).wait_send()
        for e in range(1, RING):
            y_copy(g, e).wait_send()
            z_copy(g, e).wait_send()
        last(g).wait_send()
        return carry

    lax.fori_loop(0, SLOTS, sums_settle, 0)

    def out_settle(h, carry):
        result(h).wait()
        return carry

    lax.fori_loop(0, width // HEAD, out_settle, 0)


def per_device(
    mesh, fine_x, fine_q, fine_k, fine_v, windows, pool_w, norm_gain, w_query, w_key, w_value, w_out, up_w
):
    rows, width = fine_q.shape
    kv_width = fine_k.shape[1]
    n_tp, n_ctx = mesh.shape["tp"], mesh.shape["ctx"]
    reach = WIN // rows
    span = (reach + 1) * rows
    own = rows // POOL
    all_rows = own * n_tp
    depth, q_width = w_query.shape
    heads = q_width // HEAD
    w_cols = q_width + 2 * HEAD
    dma = pltpu.SemaphoreType.DMA
    return pl.pallas_call(
        block_kernel,
        out_shape=jax.ShapeDtypeStruct((rows, width), F32),
        in_specs=[ANY_SPEC] * 4
        + [pl.BlockSpec(memory_space=pltpu.SMEM)]
        + [VMEM_SPEC] * 3
        + [ANY_SPEC] * 4,
        out_specs=ANY_SPEC,
        scratch_shapes=[
            pltpu.VMEM((rows, width), BF16),
            pltpu.VMEM((rows, width), BF16),
            pltpu.VMEM((span, kv_width), BF16),
            pltpu.VMEM((span, kv_width), BF16),
            pltpu.VMEM((rows, span), jnp.int32),
            pltpu.VMEM((width // HEAD, rows, HEAD), F32),
            pltpu.VMEM((own, width), F32),
            pltpu.VMEM((own, width), BF16),
            pltpu.VMEM((RING * all_rows, width // RING), BF16),
            pltpu.VMEM((n_tp, own, HEAD), F32),
            pltpu.VMEM((own, HEAD), F32),
            pltpu.VMEM((SLOTS * depth, w_cols), BF16),
            pltpu.VMEM((SLOTS,) + w_out.shape, BF16),
            pltpu.VMEM((3, RING, all_rows, 2 * HEAD), BF16),
            pltpu.VMEM((3, RING, all_rows, 2 * HEAD), BF16),
            pltpu.VMEM((n_ctx, all_rows, 2 * HEAD), BF16),
            pltpu.VMEM((heads, all_rows, HEAD), BF16),
            pltpu.VMEM((heads, all_rows, 1), F32),
            pltpu.VMEM((heads, all_rows, 1), F32),
            pltpu.VMEM((heads, all_rows, HEAD), F32),
            pltpu.VMEM((RING, all_rows, q_width), BF16),
        ]
        + [pltpu.VMEM((RING * all_rows // 2, width // RING), BF16)] * 5
        + [
            pltpu.VMEM((RING * own, width // RING), F32),
            pltpu.VMEM((RING * own, width // RING), BF16),
            pltpu.VMEM((RING * own, width // RING), BF16),
            pltpu.VMEM((own, width), F32),
            pltpu.VMEM((SLOTS, 8, w_out.shape[1]), F32),
            pltpu.VMEM((SLOTS, 8, w_out.shape[1]), F32),
            dma((4,)),
            dma((2, CHUNKS, reach)),
            dma((2, CHUNKS, reach)),
            dma((CHUNKS, 2)),
            dma((2, RING)),
            dma((2, RING)),
            dma((2, n_tp)),
            dma((2, RING)),
            dma((2, 2)),
            dma((2, 2)),
            dma((2, RING)),
            dma((n_tp,)),
            dma((3, 4)),
            dma((2, SLOTS, 2)),
            dma((2, SLOTS)),
            dma((3, RING)),
            dma((3, RING)),
            dma((RING,)),
            dma((RING, RING)),
            dma((RING,)),
            dma((RING, RING)),
            dma((n_ctx,)),
            dma((n_ctx,)),
            dma((heads // 2, RING)),
            dma((heads // 2, RING)),
            dma((SLOTS,)),
            dma((SLOTS,)),
            dma((SLOTS, RING)),
            dma((SLOTS, RING)),
            dma((SLOTS, RING)),
            dma((SLOTS, RING)),
            dma((2, SLOTS)),
            dma((width // HEAD,)),
        ],
        compiler_params=pltpu.CompilerParams(
            collective_id=0, has_side_effects=True, vmem_limit_bytes=62 * 2**20
        ),
        name="hourglass",
    )(
        fine_q, fine_k, fine_v, fine_x, windows, pool_w, norm_gain[None], up_w,
        w_query, w_key, w_value, w_out,
    )


def solution(mesh):
    placed = (
        P(("ctx", "tp"), None),
        P(("ctx", "tp"), None),
        P(("ctx", "tp"), None),
        P(("ctx", "tp"), None),
        P(),
        P(),
        P(),
        P("ctx", "tp"),
        P("ctx", "tp"),
        P("ctx", "tp"),
        P("tp", "ctx"),
        P(),
    )
    return jax.shard_map(
        functools.partial(per_device, mesh),
        mesh=mesh,
        in_specs=placed,
        out_specs=P(("ctx", "tp"), None),
        check_vma=False,
    )
```
